256 devices in a mesh: dp: 16 (over y, z_hi, core), mx: 4 (over z_lo), my: 4 (over x).
Axes of the slice: x: 4, y: 4, z: 8 (z_hi: 2, z_lo: 4; z = z_hi * 4 + z_lo), core: 2. Of those that a mesh axis runs over, the one named last changes fastest.
Arguments:
- features: bfloat16 [128, 128, 3072], P('dp', None, 'mx'), may hold values from -6 to 6
- segment_ids: int32 [128, 128], P('dp'), may hold values from 0 to 3, never falling along the last dimension, each value on 1 to 80 neighbouring positions
- owners: int32 [16, 8], replicated, may hold values from 0 to 15, as said below
- w_qkv: bfloat16 [3072, 9216], P('mx', 'my'), may hold values from -0.109375 to 0.109375
- w_out: bfloat16 [3072, 3072], P('my', 'mx'), may hold values from -0.109375 to 0.109375
- cotangent: bfloat16 [128, 128, 3072], P('dp', None, 'mx'), may hold values from -6 to 6
Outputs:
- grad_features: bfloat16 [128, 128, 3072], P('dp', 'my', 'mx')
- grad_qkv: float32 [4, 768, 9216], P('mx', 'dp', 'my')
- grad_out: float32 [4, 768, 3072], P('my', 'dp', 'mx')
The draws below stay inside these ranges and needn't reach their ends.
Inputs may be any that keep to these rules, and one draw needn't show every extreme that they name: For each tile position the 16 loaders send to 16 different owners, so every owner receives exactly 8 tiles; one loader sends at most 1 tiles to one owner, and some loader sends exactly 1. `segment_ids`: within a tile the ids never fall; an image covers 1 to 80 patches.
All inputs are finite; a program needn't handle non-finite values.
Results may differ from the reference program's by a relative error of at most 0.035.
Values may be sent and summed in bfloat16 or wider, within the bound.
A program may use at most 64 MiB of HBM per device.

```python
import math
import jax
import jax.numpy as jnp
import numpy as np
from jax import lax

D = 3072
HEADS = 24
HEAD = 128
P_SIZE = 128
SEGS = 4
TILES_DEV = 8
MOST = 80
TILES = 128
N_DP = 16
N_MX = 4
N_MY = 4


def draw_owners(key, part):
    key = jax.random.fold_in(key, 11)
    first_key, second_key = jax.random.split(key)
    relabel = jax.random.permutation(first_key, N_DP)
    offsets = jax.random.permutation(second_key, N_DP)
    loader = jnp.arange(N_DP)[:, None]
    position = jnp.arange(TILES_DEV)[None, :]
    return relabel[(loader + offsets[position % N_DP]) % N_DP].astype(jnp.int32)


def levels(own_key, extent, shards, least, top_value):
    loudness = 1.0
    for dim, shards_of in shards:
        heights = jax.random.uniform(jax.random.fold_in(jax.random.fold_in(own_key, 6), dim), (shards_of,), jnp.float32, least / len(shards), top_value / len(shards))
        loudness = loudness * jnp.repeat(jnp.exp(heights), extent[dim] // shards_of).reshape((-1,) + (1,) * (len(extent) - 1 - dim))
    return loudness


def profile(count, total, most, lean):
    weights = [(1 << 20) // math.isqrt(standing ** lean) + 1 for standing in range(2, count + 1)]
    spare, given = total - most - (count - 1), [1] * (count - 1)
    while spare > 0:
        free = [i for i in range(count - 1) if given[i] < most]
        pool, remaining = sum([weights[i] for i in free]), spare
        for i in free:
            extra = min(most - given[i], max(1, remaining * weights[i] // pool), spare)
            given[i] = given[i] + extra
            spare = spare - extra
    return np.array([most] + given)


def uneven_parts(key, number_of, total, limit, slope):
    if number_of == 2:
        one = jax.random.randint(key, (), max(1, total - limit), min(limit, total - 1) + 1)
        return jnp.stack([one, total - one])
    lengths = jnp.asarray(profile(number_of, total, limit, slope), jnp.int32)
    twos = (number_of - 1) // 2
    donor, receiver = lengths[1:1 + 2 * twos:2], lengths[2:2 + 2 * twos:2]
    margin = jnp.minimum(donor - 1, limit - receiver)
    shifted = jax.random.randint(jax.random.fold_in(key, 1), (twos,), 0, 1 << 20) % (margin + 1)
    lengths = lengths.at[1:1 + 2 * twos:2].set(donor - shifted).at[2:2 + 2 * twos:2].set(receiver + shifted)
    return lengths[jax.random.permutation(jax.random.fold_in(key, 2), number_of)]


def centred(rng, extent, deviation, reach, shards=(), kind=jnp.bfloat16):
    array = jax.random.normal(rng, extent, jnp.float32) * deviation
    if len(shards) > 0:
        array = levels(rng, extent, shards, -0.22, 0.18) * array
    return jnp.clip(array, min=-reach, max=reach).astype(kind)


def setup_inputs(seed: int = 0) -> dict:
    arg_keys = jax.random.split(jax.random.key(seed), 7)
    features = centred(arg_keys[0], (TILES, P_SIZE, D), 1.0, 6.0, ((0, 16), (2, 4)))
    segment_ids = jax.vmap(lambda own: jnp.searchsorted(jnp.cumsum(uneven_parts(own, SEGS, P_SIZE, MOST, 2)), jnp.arange(P_SIZE), side="right"))(jax.random.split(arg_keys[1], TILES)).reshape((TILES, P_SIZE)).astype(jnp.int32)
    owners = draw_owners(jax.random.fold_in(arg_keys[6], 71), 0)
    w_qkv = centred(arg_keys[3], (D, HEADS * 3 * HEAD), D ** -0.5, 0.109375, ((0, 4), (1, 4)))
    w_out = centred(arg_keys[4], (HEADS * HEAD, D), (HEADS * HEAD) ** -0.5, 0.109375, ((0, 4), (1, 4)))
    cotangent = centred(arg_keys[5], (TILES, P_SIZE, D), 1.0, 6.0, ((0, 16), (2, 4)))
    return {"features": features, "segment_ids": segment_ids, "owners": owners, "w_qkv": w_qkv, "w_out": w_out, "cotangent": cotangent}


def product(pattern, operand_a, operand_b):
    return jnp.einsum(pattern, operand_a.astype(jnp.float32), operand_b.astype(jnp.float32), precision=lax.Precision.HIGHEST)

def normalize(values):
    centered = values - lax.optimization_barrier(jnp.mean(values, axis=-1, keepdims=True))
    inverse = lax.rsqrt(lax.optimization_barrier(jnp.mean(centered * centered, axis=-1, keepdims=True)) + 1e-06)
    return (centered * inverse, inverse)

def norm_back(grad_hat, normed, inverse):
    return inverse * (grad_hat - lax.optimization_barrier(jnp.mean(grad_hat, axis=-1, keepdims=True)) - normed * lax.optimization_barrier(jnp.mean(grad_hat * normed, axis=-1, keepdims=True)))

def attend_both(qkv_rows, grad_rows, image_ids):
    length, breadth = qkv_rows.shape
    heads_here = breadth // (3 * HEAD)
    pieces = qkv_rows.reshape(length, heads_here, 3, HEAD)
    query_hat, query_inv = normalize(pieces[:, :, 0])
    key_hat, key_inv = normalize(pieces[:, :, 1])
    query_bf = query_hat.astype(jnp.bfloat16)
    key_bf = key_hat.astype(jnp.bfloat16)
    value_bf = pieces[:, :, 2].astype(jnp.bfloat16)
    score_scale = HEAD ** (-0.5)
    scores = product('qhe,khe->hqk', query_bf, key_bf) * score_scale
    same_image = image_ids[:, None] == image_ids[None, :]
    expo = jnp.where(same_image[None], jnp.exp(scores), 0.0)
    weights = expo / lax.optimization_barrier(jnp.sum(expo, axis=-1, keepdims=True))
    weights_bf = weights.astype(jnp.bfloat16)
    attended = product('hqk,khe->qhe', weights_bf, value_bf)
    grad_bf = grad_rows.reshape(length, heads_here, HEAD).astype(jnp.bfloat16)
    grad_value = product('hqk,qhe->khe', weights_bf, grad_bf)
    grad_weights = product('qhe,khe->hqk', grad_bf, value_bf)
    grad_scores = weights * (grad_weights - lax.optimization_barrier(jnp.sum(weights * grad_weights, axis=-1, keepdims=True))) * score_scale
    grad_scores_bf = grad_scores.astype(jnp.bfloat16)
    grad_query = norm_back(product('hqk,khe->qhe', grad_scores_bf, key_bf), query_hat, query_inv)
    grad_key = norm_back(product('hqk,qhe->khe', grad_scores_bf, query_bf), key_hat, key_inv)
    grad_qkv = jnp.stack([grad_query, grad_key, grad_value], axis=2).reshape(length, breadth).astype(jnp.bfloat16)
    return (attended.reshape(length, heads_here * HEAD).astype(jnp.bfloat16), grad_qkv)

def reference(features, segment_ids, owners, w_qkv, w_out, cotangent):
    tile_order = jnp.argsort(owners.reshape(-1), stable=True).astype(jnp.int32)
    owned_tiles = jnp.take(features, tile_order, axis=0).reshape(N_DP, TILES_DEV * P_SIZE, D)
    owned_ids = jnp.take(segment_ids, tile_order, axis=0).reshape(N_DP, TILES_DEV, P_SIZE)
    grad_tiles = cotangent.reshape(N_DP, TILES_DEV * P_SIZE, D)
    block_width = D // N_MX
    w_out_turned = jnp.transpose(w_out)

    def blocked(rows, matrix):
        running = jnp.zeros((rows.shape[0], matrix.shape[1]), jnp.float32)
        for block in range(N_MX):
            lower = block * block_width
            term = jnp.dot(rows[:, lower:lower + block_width], matrix[lower:lower + block_width], preferred_element_type=jnp.float32)
            running = running + lax.optimization_barrier(term.astype(jnp.bfloat16)).astype(jnp.float32)
        return running

    def one_owner(sums_now, owner_data):
        rows, grad_rows, image_ids = owner_data
        qkv = blocked(rows, w_qkv)
        back = blocked(grad_rows, w_out_turned)
        attended, grad_qkv = jax.vmap(attend_both)(qkv.reshape(TILES_DEV, P_SIZE, -1), back.reshape(TILES_DEV, P_SIZE, -1), image_ids)
        attended = attended.reshape(TILES_DEV * P_SIZE, -1)
        grad_qkv = grad_qkv.reshape(TILES_DEV * P_SIZE, -1)
        part_qkv = lax.dot_general(rows, grad_qkv, (((0,), (0,)), ((), ())), preferred_element_type=jnp.float32)
        part_out = lax.dot_general(attended, grad_rows, (((0,), (0,)), ((), ())), preferred_element_type=jnp.float32)
        part_qkv = lax.optimization_barrier(part_qkv.astype(jnp.bfloat16)).astype(jnp.float32)
        part_out = lax.optimization_barrier(part_out.astype(jnp.bfloat16)).astype(jnp.float32)
        grad_input = lax.dot_general(grad_qkv, w_qkv, (((1,), (1,)), ((), ())), preferred_element_type=jnp.float32).astype(jnp.bfloat16)
        return ((sums_now[0] + part_qkv, sums_now[1] + part_out), grad_input)
    initial = (jnp.zeros((D, HEADS * 3 * HEAD), jnp.float32), jnp.zeros((HEADS * HEAD, D), jnp.float32))
    (sum_qkv, sum_out), grad_inputs = lax.scan(one_owner, initial, (owned_tiles, grad_tiles, owned_ids))
    grad_features = grad_inputs.reshape(N_DP * TILES_DEV, P_SIZE, D)
    grad_qkv = (sum_qkv / N_DP).reshape(N_MX, D // N_MX, HEADS * 3 * HEAD)
    grad_out = (sum_out / N_DP).reshape(N_MY, HEADS * HEAD // N_MY, D)
    return (grad_features, grad_qkv, grad_out)
```

```python
import jax
import jax.numpy as jnp
from jax import lax
from jax.experimental import pallas as pl
from jax.experimental.pallas import tpu as pltpu
from jax.sharding import PartitionSpec as P

HEAD = 128
HEADS_HERE = 6
TILES = 8
HALF = 4
UNITS = HEADS_HERE * HALF
PATCH = 128
WIDE = 768
QKV = 3 * HEAD
UNIT = QKV + HEAD
CHUNKS = 8
BF = jnp.bfloat16
F32 = jnp.float32
MESH = pl.DeviceIdType.MESH
SCALE = HEAD ** (-0.5)


def dot(a, b, contract):
    return lax.dot_general(a, b, ((contract[0], contract[1]), ((), ())), preferred_element_type=F32)


NN = ((1,), (0,))
NT = ((1,), (1,))
TN = ((0,), (0,))


def normalize(values):
    centered = values - jnp.mean(values, axis=-1, keepdims=True)
    inverse = lax.rsqrt(jnp.mean(centered * centered, axis=-1, keepdims=True) + 1e-06)
    return centered * inverse, inverse


def norm_back(grad_hat, normed, inverse):
    return inverse * (
        grad_hat
        - jnp.mean(grad_hat, axis=-1, keepdims=True)
        - normed * jnp.mean(grad_hat * normed, axis=-1, keepdims=True)
    )


def attend(total, mask):
    query_hat, query_inv = normalize(total[:, :HEAD])
    key_hat, key_inv = normalize(total[:, HEAD : 2 * HEAD])
    query_bf = query_hat.astype(BF)
    key_bf = key_hat.astype(BF)
    value_bf = total[:, 2 * HEAD : 3 * HEAD].astype(BF)
    grad_bf = total[:, 3 * HEAD :].astype(BF)
    expo = jnp.exp(dot(query_bf, key_bf, NT) * SCALE) * mask
    weights = expo / jnp.sum(expo, axis=-1, keepdims=True)
    weights_bf = weights.astype(BF)
    attended = dot(weights_bf, value_bf, NN)
    grad_value = dot(weights_bf, grad_bf, TN)
    grad_weights = dot(grad_bf, value_bf, NT)
    grad_scores = (
        weights
        * (grad_weights - jnp.sum(weights * grad_weights, axis=-1, keepdims=True))
        * SCALE
    ).astype(BF)
    grad_query = norm_back(dot(grad_scores, key_bf, NN), query_hat, query_inv)
    grad_key = norm_back(dot(grad_scores, query_bf, TN), key_hat, key_inv)
    return jnp.concatenate([attended, grad_query, grad_key, grad_value], axis=1).astype(BF)


def branch(
    quarter, cot, w_qkv, w_out, mask,
    out_feat, out_qkv, out_out,
    feat, feat_t, part, chain, found, grads, core_in, core_sum, y_in, y_sum, z_in,
    grad_wide, feat_acc, feat_bf, feat_in,
    x_send, x_recv, b_send, b_recv, c_send, c_recv,
    core_send, core_recv, y_send, y_recv, z_send, z_recv, d_send, d_recv,
):
    dp = lax.axis_index("dp")
    mx = lax.axis_index("mx")
    my = lax.axis_index("my")
    core = lax.rem(dp, 2)
    high = lax.rem(dp // 2, 2)
    row = dp // 4
    is_end = (mx == 0) | (mx == 3)
    is_mid = (mx == 1) | (mx == 2)
    own = jnp.where(mx == 0, 0, HALF)
    other = HALF - own
    near = jnp.where(mx == 0, 1, 2)

    core_peer = (dp + 1 - 2 * core, mx, my)
    high_peer = (row * 4 + (1 - high) * 2 + core, mx, my)

    def row_peer(step):
        return (lax.rem(row + step, 4) * 4 + lax.rem(dp, 4), mx, my)

    def x_peer(step):
        return (dp, mx, lax.rem(my + step, 4))

    def along(to):
        return (dp, to, my)

    barrier = pltpu.get_barrier_semaphore()

    def greet(peer):
        pl.semaphore_signal(barrier, inc=1, device_id=peer, device_id_type=MESH)

    greet(core_peer)
    greet(high_peer)
    for step in range(1, 4):
        greet(row_peer(step))
        greet(x_peer(step))

    @pl.when(is_end)
    def _():
        greet(along(near))
        pl.semaphore_wait(barrier, 9)

    @pl.when(is_mid)
    def _():
        greet(along(mx - 1))
        greet(along(mx + 1))
        pl.semaphore_wait(barrier, 10)

    def remote(src, dst, send, recv, peer):
        return pltpu.make_async_remote_copy(
            src_ref=src, dst_ref=dst, send_sem=send, recv_sem=recv,
            device_id=peer, device_id_type=MESH,
        )

    mine = pl.ds(pl.multiple_of(my * 32, 32), 32)

    def x_copy(step):
        return remote(
            quarter, feat.at[:, mine], x_send.at[step - 1], x_recv.at[step - 1], x_peer(step)
        )

    for step in (2, 1, 3):
        x_copy(step).start()
    feat[:, mine, :] = quarter[...]
    for step in (1, 3, 2):
        x_copy(step).wait_recv()
    for step in range(1, 4):
        x_copy(step).wait_send()

    def project(unit):
        head = unit // HALF
        tile = lax.rem(unit, HALF)
        rows = jnp.concatenate([feat[tile], feat[tile + HALF]], axis=0)
        columns = pl.ds(pl.multiple_of(head * QKV, HEAD), QKV)
        product = dot(rows, w_qkv[:, columns], NN).astype(BF)
        rows = jnp.concatenate([cot[tile], cot[tile + HALF]], axis=0)
        lines = pl.ds(pl.multiple_of(head * HEAD, HEAD), HEAD)
        back = dot(rows, w_out[lines, :], NT).astype(BF)
        part[head, tile, :, :QKV] = product[:PATCH]
        part[head, tile + HALF, :, :QKV] = product[PATCH:]
        part[head, tile, :, QKV:] = back[:PATCH]
        part[head, tile + HALF, :, QKV:] = back[PATCH:]

    def b_copy(head, tile, to):
        return remote(
            part.at[head, tile], chain.at[head, tile], b_send, b_recv.at[head, tile], along(to)
        )

    def c_copy(head, tile, to):
        return remote(
            found.at[head, tile], found.at[head, tile], c_send, c_recv.at[head, tile], along(to)
        )

    @pl.when(is_end)
    def _():
        def send_out(unit, carry):
            project(unit)
            b_copy(unit // HALF, other + lax.rem(unit, HALF), near).start()
            return carry

        lax.fori_loop(0, UNITS, send_out, 0)

        def finish(unit, carry):
            head = unit // HALF
            tile = own + lax.rem(unit, HALF)
            b_copy(head, tile, near).wait_recv()
            total = part[head, tile].astype(F32) + chain[head, tile].astype(F32)
            found[head, tile] = attend(total, mask[tile])
            c_copy(head, tile, near).start()
            return carry

        lax.fori_loop(0, UNITS, finish, 0)

    @pl.when(is_mid)
    def _():
        def prepare(unit, carry):
            project(unit)
            return carry

        lax.fori_loop(0, HALF, prepare, 0)

        def pass_on(unit, carry):
            head = unit // HALF
            at = lax.rem(unit, HALF)
            for tile, to in ((at + HALF, mx + 1), (at, mx - 1)):
                b_copy(head, tile, to).wait_recv()
                part[head, tile] = (
                    part[head, tile].astype(F32) + chain[head, tile].astype(F32)
                ).astype(BF)
                b_copy(head, tile, to).start()

            @pl.when(unit + HALF < UNITS)
            def _():
                project(unit + HALF)

            return carry

        lax.fori_loop(0, UNITS, pass_on, 0)

    feat_acc[...] = jnp.zeros_like(feat_acc)

    def core_copy(chunk):
        return remote(
            grads.at[chunk, :, 1 - core], core_in.at[chunk],
            core_send.at[chunk], core_recv.at[chunk], core_peer,
        )

    def y_copy(chunk, step):
        return remote(
            core_sum.at[chunk, pl.ds(2 * lax.rem(row + step, 4), 2)], y_in.at[chunk, step - 1],
            y_send.at[chunk, step - 1], y_recv.at[chunk, step - 1], row_peer(step),
        )

    def z_copy(chunk):
        return remote(
            y_sum.at[chunk, 1 - high], z_in.at[chunk],
            z_send.at[chunk], z_recv.at[chunk], high_peer,
        )

    def stage_core(chunk):
        core_copy(chunk).wait_recv()
        core_sum[chunk] = (
            grads[chunk, :, core].astype(F32) + core_in[chunk].astype(F32)
        ).astype(BF)
        for step in (2, 1, 3):
            y_copy(chunk, step).start()

    def stage_row(chunk):
        total = core_sum[chunk, pl.ds(2 * row, 2)].astype(F32)
        for step in (1, 3, 2):
            y_copy(chunk, step).wait_recv()
            total = total + y_in[chunk, step - 1].astype(F32)
        y_sum[chunk] = total.astype(BF)
        z_copy(chunk).start()

    def stage_high(chunk):
        z_copy(chunk).wait_recv()
        return (y_sum[chunk, high].astype(F32) + z_in[chunk].astype(F32)) * (1.0 / 16.0)

    def store_qkv(chunk):
        columns = pl.ds(pl.multiple_of(chunk * QKV, HEAD), QKV)
        out_qkv[0, :, columns] = stage_high(chunk)

    def weight_step(unit, carry):
        at = lax.rem(unit, HALF)

        @pl.when(unit < UNITS)
        def _():
            head = unit // HALF

            @pl.when(is_mid)
            def _():
                for tile, to in ((at, mx + 1), (at + HALF, mx - 1)):
                    c_copy(head, tile, to).wait_recv()
                    c_copy(head, tile, to).start()

            @pl.when(is_end)
            def _():
                c_copy(head, other + at, near).wait_recv()

        @pl.when(unit < HALF)
        def _():
            for tile in range(2):
                columns = pl.ds(pl.multiple_of((2 * at + tile) * PATCH, PATCH), PATCH)
                feat_t[:, columns] = feat[2 * at + tile].T

        @pl.when(unit >= HALF)
        def _():
            head = unit // HALF - 1
            grad = found[head, :, :, HEAD:].reshape(TILES * PATCH, QKV)
            lines = pl.ds(pl.multiple_of(at * 192, 64), 192)
            piece = dot(feat_t[lines, :], grad, NN).astype(BF)
            grads[head, pl.ds(2 * at, 2)] = piece.reshape(2, 2, 48, QKV)
            tiles = pl.ds(2 * at, 2)
            columns = pl.ds(pl.multiple_of(head * QKV, HEAD), QKV)
            back = dot(
                found[head, tiles, :, HEAD:].reshape(2 * PATCH, QKV), w_qkv[:, columns], NT
            )
            feat_acc[tiles] += back.reshape(2, PATCH, WIDE)

            @pl.when(at == 0)
            def _():
                lines = pl.ds(pl.multiple_of(head * HEAD, HEAD), HEAD)
                grad_wide[lines, :] = dot(
                    found[head, :, :, :HEAD].reshape(TILES * PATCH, HEAD),
                    cot[...].reshape(TILES * PATCH, WIDE),
                    TN,
                ).astype(BF)

            @pl.when((at == 1) & (head >= 1))
            def _():
                stage_core(head - 1)

            @pl.when((at == 2) & (head >= 2))
            def _():
                stage_row(head - 2)

            @pl.when((at == 3) & (head >= 3))
            def _():
                store_qkv(head - 3)

            @pl.when(at == 3)
            def _():
                core_copy(head).start()

        return carry

    lax.fori_loop(0, UNITS + HALF, weight_step, 0)

    for half in range(2):
        columns = slice(half * QKV, (half + 1) * QKV)
        grads[6 + half] = grad_wide[:, columns].reshape(8, 2, 48, QKV)
        core_copy(6 + half).start()

    def d_copy(step):
        lines = pl.ds(pl.multiple_of(lax.rem(my + step, 4) * 32, 32), 32)
        return remote(
            feat_bf.at[:, lines], feat_in.at[step - 1],
            d_send.at[step - 1], d_recv.at[step - 1], x_peer(step),
        )

    feat_bf[...] = feat_acc[...].astype(BF)
    for step in (2, 1, 3):
        d_copy(step).start()
    stage_core(5)
    stage_row(4)
    stage_core(6)
    stage_core(7)
    stage_row(5)
    store_qkv(3)
    store_qkv(4)
    stage_row(6)
    stage_row(7)
    store_qkv(5)
    total = feat_acc[:, mine, :]
    for step in (1, 3, 2):
        d_copy(step).wait_recv()
        total = total + feat_in[step - 1].astype(F32)
    out_feat[...] = total.astype(BF)
    out_out[0, :, :QKV] = stage_high(6)
    out_out[0, :, QKV:] = stage_high(7)

    for step in range(1, 4):
        d_copy(step).wait_send()

    def drain(chunk, carry):
        core_copy(chunk).wait_send()
        z_copy(chunk).wait_send()
        for step in range(1, 4):
            y_copy(chunk, step).wait_send()
        return carry

    lax.fori_loop(0, CHUNKS, drain, 0)

    @pl.when(is_end)
    def _():
        sent = part.at[:, :HALF]
        pltpu.make_async_copy(sent, sent, b_send).wait()
        pltpu.make_async_copy(sent, sent, c_send).wait()

    @pl.when(is_mid)
    def _():
        pltpu.make_async_copy(part, part, b_send).wait()
        pltpu.make_async_copy(part, part, c_send).wait()


def fused(quarter, cot, w_qkv, w_out, mask):
    vmem = pl.BlockSpec(memory_space=pltpu.VMEM)
    dma = pltpu.SemaphoreType.DMA
    units = (HEADS_HERE, TILES, PATCH, UNIT)
    return pl.pallas_call(
        branch,
        out_shape=(
            jax.ShapeDtypeStruct((TILES, 32, WIDE), BF),
            jax.ShapeDtypeStruct((1, 48, HEADS_HERE * QKV), F32),
            jax.ShapeDtypeStruct((1, 48, WIDE), F32),
        ),
        in_specs=[vmem] * 5,
        out_specs=(vmem,) * 3,
        scratch_shapes=[
            pltpu.VMEM((TILES, PATCH, WIDE), BF),
            pltpu.VMEM((WIDE, TILES * PATCH), BF),
            pltpu.VMEM(units, BF),
            pltpu.VMEM(units, BF),
            pltpu.VMEM(units, BF),
            pltpu.VMEM((CHUNKS, 8, 2, 48, QKV), BF),
            pltpu.VMEM((CHUNKS, 8, 48, QKV), BF),
            pltpu.VMEM((CHUNKS, 8, 48, QKV), BF),
            pltpu.VMEM((CHUNKS, 3, 2, 48, QKV), BF),
            pltpu.VMEM((CHUNKS, 2, 48, QKV), BF),
            pltpu.VMEM((CHUNKS, 48, QKV), BF),
            pltpu.VMEM((WIDE, WIDE), BF),
            pltpu.VMEM((TILES, PATCH, WIDE), F32),
            pltpu.VMEM((TILES, PATCH, WIDE), BF),
            pltpu.VMEM((3, TILES, 32, WIDE), BF),
            dma((3,)), dma((3,)),
            dma, dma((HEADS_HERE, TILES)),
            dma, dma((HEADS_HERE, TILES)),
            dma((CHUNKS,)), dma((CHUNKS,)),
            dma((CHUNKS, 3)), dma((CHUNKS, 3)),
            dma((CHUNKS,)), dma((CHUNKS,)),
            dma((3,)), dma((3,)),
        ],
        compiler_params=pltpu.CompilerParams(
            collective_id=0, has_side_effects=True, vmem_limit_bytes=60 * 1024 * 1024
        ),
        cost_estimate=pl.CostEstimate(
            flops=14_000_000_000, bytes_accessed=12_000_000, transcendentals=400_000
        ),
    )(quarter, cot, w_qkv, w_out, mask)


def shards(features, segment_ids, owners, w_qkv, w_out, cotangent):
    me = lax.axis_index("dp")
    my = lax.axis_index("my")
    groups = lax.axis_size("dp")
    own_row = lax.dynamic_slice_in_dim(owners, me, 1, 0)[0]
    positions = jnp.arange(TILES)
    chosen = jnp.sum(
        jnp.where(own_row[None, :] == jnp.arange(groups)[:, None], positions[None, :], 0), axis=1
    )
    quarter = lax.dynamic_slice_in_dim(features, my * 32, 32, 1)
    send_rows = jnp.take(quarter, chosen, axis=0)
    got_rows = lax.all_to_all(send_rows, "dp", split_axis=0, concat_axis=0, tiled=True)
    all_ids = lax.all_gather(segment_ids, "dp", axis=0, tiled=True)
    mine = (owners == me).reshape(-1)
    rank = jnp.cumsum(mine.astype(jnp.int32)) - 1
    listed = jnp.sum(
        jnp.where(
            mine[None, :] & (rank[None, :] == positions[:, None]),
            jnp.arange(groups * TILES)[None, :],
            0,
        ),
        axis=1,
    )
    quarter = jnp.take(got_rows, listed // TILES, axis=0)
    ids = jnp.take(all_ids, listed, axis=0)
    mask = (ids[:, :, None] == ids[:, None, :]).astype(F32)
    return fused(quarter, cotangent, w_qkv, w_out, mask)


def solution(mesh):
    return jax.shard_map(
        shards,
        mesh=mesh,
        in_specs=(
            P("dp", None, "mx"),
            P("dp", None),
            P(),
            P("mx", "my"),
            P("my", "mx"),
            P("dp", None, "mx"),
        ),
        out_specs=(P("dp", "my", "mx"), P("mx", "dp", "my"), P("my", "dp", "mx")),
        check_vma=False,
    )
```

```python
import jax
import jax.numpy as jnp
from jax import lax
from jax.experimental import pallas as pl
from jax.experimental.pallas import tpu as pltpu
from jax.sharding import PartitionSpec as P

HEAD = 128
HEADS_HERE = 6
TILES = 8
HALF = 4
UNITS = HEADS_HERE * HALF
PATCH = 128
WIDE = 768
QKV = 3 * HEAD
UNIT = QKV + HEAD
CHUNKS = 8
AHEAD = 6
SLOTS = 2
LAG = 2
BF = jnp.bfloat16
F32 = jnp.float32
MESH = pl.DeviceIdType.MESH
SCALE = HEAD ** (-0.5)


def dot(a, b, contract):
    return lax.dot_general(a, b, ((contract[0], contract[1]), ((), ())), preferred_element_type=F32)


NN = ((1,), (0,))
NT = ((1,), (1,))
TN = ((0,), (0,))


def normalize(values):
    centered = values - jnp.mean(values, axis=-1, keepdims=True)
    inverse = lax.rsqrt(jnp.mean(centered * centered, axis=-1, keepdims=True) + 1e-06)
    return centered * inverse, inverse


def norm_back(grad_hat, normed, inverse):
    return inverse * (
        grad_hat
        - jnp.mean(grad_hat, axis=-1, keepdims=True)
        - normed * jnp.mean(grad_hat * normed, axis=-1, keepdims=True)
    )


def attend(total, mask):
    query_hat, query_inv = normalize(total[:, :HEAD])
    key_hat, key_inv = normalize(total[:, HEAD : 2 * HEAD])
    query_bf = query_hat.astype(BF)
    key_bf = key_hat.astype(BF)
    value_bf = total[:, 2 * HEAD : 3 * HEAD].astype(BF)
    grad_bf = total[:, 3 * HEAD :].astype(BF)
    expo = jnp.exp(dot(query_bf, key_bf, NT) * SCALE) * mask
    weights = expo / jnp.sum(expo, axis=-1, keepdims=True)
    weights_bf = weights.astype(BF)
    attended = dot(weights_bf, value_bf, NN)
    grad_value = dot(weights_bf, grad_bf, TN)
    grad_weights = dot(grad_bf, value_bf, NT)
    grad_scores = (
        weights
        * (grad_weights - jnp.sum(weights * grad_weights, axis=-1, keepdims=True))
        * SCALE
    ).astype(BF)
    grad_query = norm_back(dot(grad_scores, key_bf, NN), query_hat, query_inv)
    grad_key = norm_back(dot(grad_scores, query_bf, TN), key_hat, key_inv)
    return jnp.concatenate([attended, grad_query, grad_key, grad_value], axis=1).astype(BF)


def branch(
    quarter, cot, w_qkv, w_out, mask,
    out_feat, out_qkv, out_out,
    feat, feat_t, part, chain, found, grads, core_in, core_sum, y_in, y_sum, z_in,
    grad_wide, feat_acc, feat_bf, feat_in,
    x_send, x_recv, b_send, b_recv, c_recv,
    core_send, core_recv, y_send, y_recv, z_send, z_recv, d_send, d_recv,
):
    dp = lax.axis_index("dp")
    mx = lax.axis_index("mx")
    my = lax.axis_index("my")
    core = lax.rem(dp, 2)
    high = lax.rem(dp // 2, 2)
    row = dp // 4
    is_end = (mx == 0) | (mx == 3)
    is_mid = (mx == 1) | (mx == 2)
    own = jnp.where(mx == 0, 0, HALF)
    other = HALF - own
    near = jnp.where(mx == 0, 1, 2)
    middle = 3 - mx
    edge = jnp.where(mx == 1, 0, 3)
    edge_base = jnp.where(mx == 1, 0, HALF)
    far_base = HALF - edge_base

    core_peer = (dp + 1 - 2 * core, mx, my)
    high_peer = (row * 4 + (1 - high) * 2 + core, mx, my)

    def row_peer(step):
        return (lax.rem(row + step, 4) * 4 + lax.rem(dp, 4), mx, my)

    def x_peer(step):
        return (dp, mx, lax.rem(my + step, 4))

    def along(to):
        return (dp, to, my)

    barrier = pltpu.get_barrier_semaphore()

    def greet(peer):
        pl.semaphore_signal(barrier, inc=1, device_id=peer, device_id_type=MESH)

    greet(core_peer)
    greet(high_peer)
    for step in range(1, 4):
        greet(row_peer(step))
        greet(x_peer(step))

    @pl.when(is_end)
    def _():
        greet(along(near))
        pl.semaphore_wait(barrier, 9)

    @pl.when(is_mid)
    def _():
        greet(along(mx - 1))
        greet(along(mx + 1))
        pl.semaphore_wait(barrier, 10)

    def remote(src, dst, send, recv, peer):
        return pltpu.make_async_remote_copy(
            src_ref=src, dst_ref=dst, send_sem=send, recv_sem=recv,
            device_id=peer, device_id_type=MESH,
        )

    mine = pl.ds(pl.multiple_of(my * 32, 32), 32)

    def x_copy(step):
        return remote(
            quarter, feat.at[:, mine], x_send.at[step - 1], x_recv.at[step - 1], x_peer(step)
        )

    for step in (2, 1, 3):
        x_copy(step).start()
    feat[:, mine, :] = quarter[...]
    for step in (1, 3, 2):
        x_copy(step).wait_recv()
    for step in range(1, 4):
        x_copy(step).wait_send()

    def project(unit):
        head = unit // HALF
        tile = lax.rem(unit, HALF)
        rows = jnp.concatenate([feat[tile], feat[tile + HALF]], axis=0)
        columns = pl.ds(pl.multiple_of(head * QKV, HEAD), QKV)
        product = dot(rows, w_qkv[:, columns], NN).astype(BF)
        rows = jnp.concatenate([cot[tile], cot[tile + HALF]], axis=0)
        lines = pl.ds(pl.multiple_of(head * HEAD, HEAD), HEAD)
        back = dot(rows, w_out[lines, :], NT).astype(BF)
        part[head, tile, :, :QKV] = product[:PATCH]
        part[head, tile + HALF, :, :QKV] = product[PATCH:]
        part[head, tile, :, QKV:] = back[:PATCH]
        part[head, tile + HALF, :, QKV:] = back[PATCH:]

    def b_copy(head, tile, to, slot):
        return remote(
            part.at[head, tile], chain.at[head, tile],
            b_send.at[slot], b_recv.at[head, tile], along(to),
        )

    def c_copy(head, tile, to, slot):
        return remote(
            found.at[head, tile], found.at[head, tile],
            b_send.at[slot], c_recv.at[head, tile], along(to),
        )

    def slot_of(unit, stream=0):
        return stream * SLOTS + lax.rem(unit, SLOTS)

    def b_out(unit):
        return b_copy(unit // HALF, other + lax.rem(unit, HALF), near, slot_of(unit))

    def c_out(unit):
        return c_copy(unit // HALF, own + lax.rem(unit, HALF), near, slot_of(unit))

    def free(unit, stream=0):
        b_copy(0, 0, near, slot_of(unit, stream)).wait_send()

    @pl.when(is_end)
    def _():
        def send_out(unit, carry):
            project(unit)

            @pl.when(unit >= SLOTS)
            def _():
                free(unit)

            b_out(unit).start()
            return carry

        lax.fori_loop(0, AHEAD, send_out, 0)

        def finish(unit, carry):
            head = unit // HALF
            tile = own + lax.rem(unit, HALF)
            b_copy(head, tile, near, 0).wait_recv()
            total = part[head, tile].astype(F32) + chain[head, tile].astype(F32)
            found[head, tile] = attend(total, mask[tile])
            later = unit + AHEAD

            @pl.when(later < UNITS)
            def _():
                project(later)
                free(later)
                b_out(later).start()

            @pl.when(later >= UNITS)
            def _():
                free(later)
                c_out(later - UNITS).start()

            return carry

        lax.fori_loop(0, UNITS, finish, 0)

    @pl.when(is_mid)
    def _():
        def prepare(unit, carry):
            project(unit)
            return carry

        lax.fori_loop(0, HALF, prepare, 0)

        def add_on(unit, base, to, stream):
            head = unit // HALF
            tile = base + lax.rem(unit, HALF)
            b_copy(head, tile, to, 0).wait_recv()
            part[head, tile] = (
                part[head, tile].astype(F32) + chain[head, tile].astype(F32)
            ).astype(BF)

            @pl.when(unit >= SLOTS)
            def _():
                free(unit, stream)

            b_copy(head, tile, to, slot_of(unit, stream)).start()

        def pass_on(unit, carry):
            @pl.when(unit < UNITS)
            def _():
                add_on(unit, far_base, middle, 0)

            @pl.when(unit >= LAG)
            def _():
                add_on(unit - LAG, edge_base, edge, 1)

            @pl.when(unit + HALF < UNITS)
            def _():
                project(unit + HALF)

            return carry

        lax.fori_loop(0, UNITS + LAG, pass_on, 0)

    feat_acc[...] = jnp.zeros_like(feat_acc)

    def core_copy(chunk):
        return remote(
            grads.at[chunk, :, 1 - core], core_in.at[chunk],
            core_send.at[chunk], core_recv.at[chunk], core_peer,
        )

    def y_copy(chunk, step):
        return remote(
            core_sum.at[chunk, pl.ds(2 * lax.rem(row + step, 4), 2)], y_in.at[chunk, step - 1],
            y_send.at[chunk, step - 1], y_recv.at[chunk, step - 1], row_peer(step),
        )

    def z_copy(chunk):
        return remote(
            y_sum.at[chunk, 1 - high], z_in.at[chunk],
            z_send.at[chunk], z_recv.at[chunk], high_peer,
        )

    def stage_core(chunk):
        core_copy(chunk).wait_recv()
        core_sum[chunk] = (
            grads[chunk, :, core].astype(F32) + core_in[chunk].astype(F32)
        ).astype(BF)
        for step in (2, 1, 3):
            y_copy(chunk, step).start()

    def stage_row(chunk):
        total = core_sum[chunk, pl.ds(2 * row, 2)].astype(F32)
        for step in (1, 3, 2):
            y_copy(chunk, step).wait_recv()
            total = total + y_in[chunk, step - 1].astype(F32)
        y_sum[chunk] = total.astype(BF)
        z_copy(chunk).start()

    def stage_high(chunk):
        z_copy(chunk).wait_recv()
        return (y_sum[chunk, high].astype(F32) + z_in[chunk].astype(F32)) * (1.0 / 16.0)

    def store_qkv(chunk):
        columns = pl.ds(pl.multiple_of(chunk * QKV, HEAD), QKV)
        out_qkv[0, :, columns] = stage_high(chunk)

    def hand_on(unit, base, to, stream):
        head = unit // HALF
        tile = base + lax.rem(unit, HALF)
        c_copy(head, tile, to, 0).wait_recv()
        free(unit, stream)
        c_copy(head, tile, to, slot_of(unit, stream)).start()

    def weight_step(unit, carry):
        @pl.when(is_mid)
        def _():
            @pl.when(unit < UNITS)
            def _():
                hand_on(unit, edge_base, middle, 0)

            @pl.when((unit >= LAG) & (unit < UNITS + LAG))
            def _():
                hand_on(unit - LAG, far_base, edge, 1)

        @pl.when(is_end)
        def _():
            @pl.when(unit + AHEAD < UNITS)
            def _():
                free(unit + AHEAD)
                c_out(unit + AHEAD).start()

            @pl.when((unit >= LAG) & (unit < UNITS + LAG))
            def _():
                got = unit - LAG
                c_copy(got // HALF, other + lax.rem(got, HALF), near, 0).wait_recv()

        @pl.when(unit < HALF)
        def _():
            for tile in range(2):
                columns = pl.ds(pl.multiple_of((2 * unit + tile) * PATCH, PATCH), PATCH)
                feat_t[:, columns] = feat[2 * unit + tile].T

        @pl.when(unit >= HALF - 1 + LAG)
        def _():
            done = unit - (HALF - 1 + LAG)
            head = done // HALF
            at = lax.rem(done, HALF)
            grad = found[head, :, :, HEAD:].reshape(TILES * PATCH, QKV)
            lines = pl.ds(pl.multiple_of(at * 192, 64), 192)
            piece = dot(feat_t[lines, :], grad, NN).astype(BF)
            grads[head, pl.ds(2 * at, 2)] = piece.reshape(2, 2, 48, QKV)
            tiles = pl.ds(2 * at, 2)
            columns = pl.ds(pl.multiple_of(head * QKV, HEAD), QKV)
            back = dot(
                found[head, tiles, :, HEAD:].reshape(2 * PATCH, QKV), w_qkv[:, columns], NT
            )
            feat_acc[tiles] += back.reshape(2, PATCH, WIDE)

            @pl.when(at == 0)
            def _():
                lines = pl.ds(pl.multiple_of(head * HEAD, HEAD), HEAD)
                grad_wide[lines, :] = dot(
                    found[head, :, :, :HEAD].reshape(TILES * PATCH, HEAD),
                    cot[...].reshape(TILES * PATCH, WIDE),
                    TN,
                ).astype(BF)

            @pl.when((at == 1) & (head >= 1))
            def _():
                stage_core(head - 1)

            @pl.when((at == 2) & (head >= 2))
            def _():
                stage_row(head - 2)

            @pl.when((at == 3) & (head >= 3))
            def _():
                store_qkv(head - 3)

            @pl.when(at == 3)
            def _():
                core_copy(head).start()

        return carry

    lax.fori_loop(0, UNITS + HALF - 1 + LAG, weight_step, 0)

    for half in range(2):
        columns = slice(half * QKV, (half + 1) * QKV)
        grads[6 + half] = grad_wide[:, columns].reshape(8, 2, 48, QKV)
        core_copy(6 + half).start()

    def d_copy(step):
        lines = pl.ds(pl.multiple_of(lax.rem(my + step, 4) * 32, 32), 32)
        return remote(
            feat_bf.at[:, lines], feat_in.at[step - 1],
            d_send.at[step - 1], d_recv.at[step - 1], x_peer(step),
        )

    feat_bf[...] = feat_acc[...].astype(BF)
    for step in (2, 1, 3):
        d_copy(step).start()
    stage_core(5)
    stage_row(4)
    stage_core(6)
    stage_core(7)
    stage_row(5)
    store_qkv(3)
    store_qkv(4)
    stage_row(6)
    stage_row(7)
    store_qkv(5)
    total = feat_acc[:, mine, :]
    for step in (1, 3, 2):
        d_copy(step).wait_recv()
        total = total + feat_in[step - 1].astype(F32)
    out_feat[...] = total.astype(BF)
    out_out[0, :, :QKV] = stage_high(6)
    out_out[0, :, QKV:] = stage_high(7)

    for step in range(1, 4):
        d_copy(step).wait_send()

    def drain(chunk, carry):
        core_copy(chunk).wait_send()
        z_copy(chunk).wait_send()
        for step in range(1, 4):
            y_copy(chunk, step).wait_send()
        return carry

    lax.fori_loop(0, CHUNKS, drain, 0)

    for slot in range(SLOTS):
        free(slot)

    @pl.when(is_mid)
    def _():
        for slot in range(SLOTS):
            free(slot, 1)


def fused(quarter, cot, w_qkv, w_out, mask):
    vmem = pl.BlockSpec(memory_space=pltpu.VMEM)
    dma = pltpu.SemaphoreType.DMA
    units = (HEADS_HERE, TILES, PATCH, UNIT)
    return pl.pallas_call(
        branch,
        out_shape=(
            jax.ShapeDtypeStruct((TILES, 32, WIDE), BF),
            jax.ShapeDtypeStruct((1, 48, HEADS_HERE * QKV), F32),
            jax.ShapeDtypeStruct((1, 48, WIDE), F32),
        ),
        in_specs=[vmem] * 5,
        out_specs=(vmem,) * 3,
        scratch_shapes=[
            pltpu.VMEM((TILES, PATCH, WIDE), BF),
            pltpu.VMEM((WIDE, TILES * PATCH), BF),
            pltpu.VMEM(units, BF),
            pltpu.VMEM(units, BF),
            pltpu.VMEM(units, BF),
            pltpu.VMEM((CHUNKS, 8, 2, 48, QKV), BF),
            pltpu.VMEM((CHUNKS, 8, 48, QKV), BF),
            pltpu.VMEM((CHUNKS, 8, 48, QKV), BF),
            pltpu.VMEM((CHUNKS, 3, 2, 48, QKV), BF),
            pltpu.VMEM((CHUNKS, 2, 48, QKV), BF),
            pltpu.VMEM((CHUNKS, 48, QKV), BF),
            pltpu.VMEM((WIDE, WIDE), BF),
            pltpu.VMEM((TILES, PATCH, WIDE), F32),
            pltpu.VMEM((TILES, PATCH, WIDE), BF),
            pltpu.VMEM((3, TILES, 32, WIDE), BF),
            dma((3,)), dma((3,)),
            dma((2 * SLOTS,)), dma((HEADS_HERE, TILES)), dma((HEADS_HERE, TILES)),
            dma((CHUNKS,)), dma((CHUNKS,)),
            dma((CHUNKS, 3)), dma((CHUNKS, 3)),
            dma((CHUNKS,)), dma((CHUNKS,)),
            dma((3,)), dma((3,)),
        ],
        compiler_params=pltpu.CompilerParams(
            collective_id=0, has_side_effects=True, vmem_limit_bytes=60 * 1024 * 1024
        ),
        cost_estimate=pl.CostEstimate(
            flops=14_000_000_000, bytes_accessed=12_000_000, transcendentals=400_000
        ),
    )(quarter, cot, w_qkv, w_out, mask)


def shards(features, segment_ids, owners, w_qkv, w_out, cotangent):
    me = lax.axis_index("dp")
    my = lax.axis_index("my")
    groups = lax.axis_size("dp")
    own_row = lax.dynamic_slice_in_dim(owners, me, 1, 0)[0]
    positions = jnp.arange(TILES)
    chosen = jnp.sum(
        jnp.where(own_row[None, :] == jnp.arange(groups)[:, None], positions[None, :], 0), axis=1
    )
    quarter = lax.dynamic_slice_in_dim(features, my * 32, 32, 1)
    send_rows = jnp.take(quarter, chosen, axis=0)
    got_rows = lax.all_to_all(send_rows, "dp", split_axis=0, concat_axis=0, tiled=True)
    all_ids = lax.all_gather(segment_ids, "dp", axis=0, tiled=True)
    mine = (owners == me).reshape(-1)
    rank = jnp.cumsum(mine.astype(jnp.int32)) - 1
    listed = jnp.sum(
        jnp.where(
            mine[None, :] & (rank[None, :] == positions[:, None]),
            jnp.arange(groups * TILES)[None, :],
            0,
        ),
        axis=1,
    )
    quarter = jnp.take(got_rows, listed // TILES, axis=0)
    ids = jnp.take(all_ids, listed, axis=0)
    mask = (ids[:, :, None] == ids[:, None, :]).astype(F32)
    return fused(quarter, cotangent, w_qkv, w_out, mask)


def solution(mesh):
    return jax.shard_map(
        shards,
        mesh=mesh,
        in_specs=(
            P("dp", None, "mx"),
            P("dp", None),
            P(),
            P("mx", "my"),
            P("my", "mx"),
            P("dp", None, "mx"),
        ),
        out_specs=(P("dp", "my", "mx"), P("mx", "dp", "my"), P("my", "dp", "mx")),
        check_vma=False,
    )
```

```python
import jax
import jax.numpy as jnp
from jax import lax
from jax.experimental import pallas as pl
from jax.experimental.pallas import tpu as pltpu
from jax.sharding import PartitionSpec as P

HEAD = 128
HEADS_HERE = 6
TILES = 8
HALF = 4
UNITS = HEADS_HERE * HALF
GROUPS = HEADS_HERE + 2
SUMS = GROUPS * HALF
BACKS = 2 * HALF
LOADERS = 16
QUARTER = 32
PATCH = 128
WIDE = 768
QKV = 3 * HEAD
UNIT = QKV + HEAD
CHUNKS = 8
AHEAD = 6
SLOTS = 2
LAG = 2
BF = jnp.bfloat16
F32 = jnp.float32
MESH = pl.DeviceIdType.MESH
SCALE = HEAD ** (-0.5)


def dot(a, b, contract):
    return lax.dot_general(a, b, ((contract[0], contract[1]), ((), ())), preferred_element_type=F32)


NN = ((1,), (0,))
NT = ((1,), (1,))
TN = ((0,), (0,))


def normalize(values):
    centered = values - jnp.mean(values, axis=-1, keepdims=True)
    inverse = lax.rsqrt(jnp.mean(centered * centered, axis=-1, keepdims=True) + 1e-06)
    return centered * inverse, inverse


def norm_back(grad_hat, normed, inverse):
    return inverse * (
        grad_hat
        - jnp.mean(grad_hat, axis=-1, keepdims=True)
        - normed * jnp.mean(grad_hat * normed, axis=-1, keepdims=True)
    )


def attend(total, grad_bf, mask):
    query_hat, query_inv = normalize(total[:, :HEAD])
    key_hat, key_inv = normalize(total[:, HEAD : 2 * HEAD])
    query_bf = query_hat.astype(BF)
    key_bf = key_hat.astype(BF)
    value_bf = total[:, 2 * HEAD :].astype(BF)
    expo = jnp.exp(dot(query_bf, key_bf, NT) * SCALE) * mask
    weights = expo / jnp.sum(expo, axis=-1, keepdims=True)
    weights_bf = weights.astype(BF)
    attended = dot(weights_bf, value_bf, NN)
    grad_value = dot(weights_bf, grad_bf, TN)
    grad_weights = dot(grad_bf, value_bf, NT)
    grad_scores = (
        weights
        * (grad_weights - jnp.sum(weights * grad_weights, axis=-1, keepdims=True))
        * SCALE
    ).astype(BF)
    grad_query = norm_back(dot(grad_scores, key_bf, NN), query_hat, query_inv)
    grad_key = norm_back(dot(grad_scores, query_bf, TN), key_hat, key_inv)
    return jnp.concatenate([attended, grad_query, grad_key, grad_value], axis=1).astype(BF)


def branch(
    owners, given, given_ids, cot, w_qkv, w_out,
    out_feat, out_qkv, out_out,
    feat, feat_t, part, chain, found, grads, core_in, core_sum, y_in, y_sum, z_in,
    grad_wide, feat_acc, feat_bf, feat_in, outbox, inbox, ids, mask,
    a_send, a_recv, i_send, i_recv, x_send, x_recv, b_send, b_recv, c_send, c_recv,
    core_send, core_recv, y_send, y_recv, z_send, z_recv, d_send, d_recv,
):
    dp = lax.axis_index("dp")
    mx = lax.axis_index("mx")
    my = lax.axis_index("my")
    core = lax.rem(dp, 2)
    high = lax.rem(dp // 2, 2)
    row = dp // 4
    is_end = (mx == 0) | (mx == 3)
    is_mid = (mx == 1) | (mx == 2)
    own = jnp.where(mx == 0, 0, HALF)
    other = HALF - own
    near = jnp.where(mx == 0, 1, 2)
    middle = 3 - mx
    edge = jnp.where(mx == 1, 0, 3)
    edge_base = jnp.where(mx == 1, 0, HALF)
    far_base = HALF - edge_base

    core_peer = (dp + 1 - 2 * core, mx, my)
    high_peer = (row * 4 + (1 - high) * 2 + core, mx, my)

    def row_peer(step):
        return (lax.rem(row + step, 4) * 4 + lax.rem(dp, 4), mx, my)

    def x_peer(step):
        return (dp, mx, lax.rem(my + step, 4))

    def along(to):
        return (dp, to, my)

    barrier = pltpu.get_barrier_semaphore()

    def greet(peer):
        pl.semaphore_signal(barrier, inc=1, device_id=peer, device_id_type=MESH)

    def dp_peer(step):
        return (lax.rem(dp + step, LOADERS), mx, my)

    for step in range(1, LOADERS):
        greet(dp_peer(step))
    for step in range(1, 4):
        greet(x_peer(step))

    @pl.when(is_end)
    def _():
        greet(along(near))
        pl.semaphore_wait(barrier, 19)

    @pl.when(is_mid)
    def _():
        greet(along(mx - 1))
        greet(along(mx + 1))
        pl.semaphore_wait(barrier, 20)

    def remote(src, dst, send, recv, peer):
        return pltpu.make_async_remote_copy(
            src_ref=src, dst_ref=dst, send_sem=send, recv_sem=recv,
            device_id=peer, device_id_type=MESH,
        )

    mine = pl.ds(pl.multiple_of(my * QUARTER, QUARTER), QUARTER)

    def position(loader, owner):
        place = jnp.int32(0)
        for tile in range(TILES):
            place = jnp.where(owners[loader, tile] == owner, tile, place)
        return place

    def fill(owner, carry):
        outbox[owner] = given[position(dp, owner), mine, :]
        return carry

    lax.fori_loop(0, LOADERS, fill, 0)

    def a_copy(step):
        return remote(
            outbox.at[lax.rem(dp + step, LOADERS)], inbox.at[dp],
            a_send.at[step - 1], a_recv.at[step - 1], dp_peer(step),
        )

    def i_copy(step):
        return remote(
            given_ids, ids.at[dp], i_send.at[step - 1], i_recv.at[step - 1], dp_peer(step)
        )

    for step in (2, 6, 10, 14, 1, 3, 5, 7, 9, 11, 13, 15, 4, 12, 8):
        a_copy(step).start()
        i_copy(step).start()
    inbox[dp] = outbox[dp]
    ids[dp] = given_ids[...]

    loaders = [jnp.int32(0)] * TILES
    places = [jnp.int32(0)] * TILES
    count = jnp.int32(0)
    for loader in range(LOADERS):
        here = jnp.int32(0)
        for tile in range(TILES):
            here = jnp.where(owners[loader, tile] == dp, 1, here)
        place = position(loader, dp)
        for tile in range(TILES):
            fits = (here > 0) & (count == tile)
            loaders[tile] = jnp.where(fits, loader, loaders[tile])
            places[tile] = jnp.where(fits, place, places[tile])
        count = count + here

    def x_copy(step):
        return remote(
            feat.at[:, mine], feat.at[:, mine],
            x_send.at[step - 1], x_recv.at[step - 1], x_peer(step),
        )

    def take_tiles():
        for step in range(1, LOADERS):
            a_copy(step).wait_recv()
        for tile in range(TILES):
            feat[tile, mine, :] = inbox[loaders[tile]]
        for step in (2, 1, 3):
            x_copy(step).start()

    def take_quarters():
        for step in (1, 3, 2):
            x_copy(step).wait_recv()

    def make_masks():
        for step in range(1, LOADERS):
            i_copy(step).wait_recv()
        for tile in range(HALF):
            loader = jnp.where(mx == 0, loaders[tile], loaders[tile + HALF])
            place = jnp.where(mx == 0, places[tile], places[tile + HALF])
            line = ids[loader, pl.ds(place, 1), :].astype(F32)
            across = jnp.broadcast_to(line, (PATCH, PATCH))
            mask[tile] = (across == across.T).astype(F32)

    def project_back(unit):
        half = unit // HALF
        tile = lax.rem(unit, HALF)
        rows = jnp.concatenate([cot[tile], cot[tile + HALF]], axis=0)
        lines = pl.ds(pl.multiple_of(half * QKV, HEAD), QKV)
        product = dot(rows, w_out[lines, :], NT).astype(BF)
        part[half, tile] = product[:PATCH]
        part[half, tile + HALF] = product[PATCH:]

    def project(unit):
        group = unit // HALF
        tile = lax.rem(unit, HALF)
        rows = jnp.concatenate([feat[tile], feat[tile + HALF]], axis=0)
        columns = pl.ds(pl.multiple_of((group - 2) * QKV, HEAD), QKV)
        product = dot(rows, w_qkv[:, columns], NN).astype(BF)
        part[group, tile] = product[:PATCH]
        part[group, tile + HALF] = product[PATCH:]

    def run(function, start, stop):
        def step(unit, carry):
            function(unit)
            return carry

        lax.fori_loop(start, stop, step, 0)

    def b_copy(head, tile, to, slot):
        return remote(
            part.at[head, tile], chain.at[head, tile],
            b_send.at[slot], b_recv.at[head, tile], along(to),
        )

    def c_copy(head, tile, to, slot):
        return remote(
            found.at[head, tile], found.at[head, tile],
            c_send.at[slot], c_recv.at[head, tile], along(to),
        )

    def slot_of(unit, stream=0):
        return stream * SLOTS + lax.rem(unit, SLOTS)

    def b_out(unit):
        return b_copy(unit // HALF, other + lax.rem(unit, HALF), near, slot_of(unit))

    def c_out(unit):
        return c_copy(unit // HALF, own + lax.rem(unit, HALF), near, slot_of(unit))

    def b_free(unit, stream=0):
        b_copy(0, 0, near, slot_of(unit, stream)).wait_send()

    def c_free(unit, stream=0):
        c_copy(0, 0, near, slot_of(unit, stream)).wait_send()

    @pl.when(is_end)
    def _():
        run(project_back, 0, BACKS)

        def send_out(unit):
            @pl.when(unit >= SLOTS)
            def _():
                b_free(unit)

            b_out(unit).start()

        def finish(unit):
            group = unit // HALF
            at = lax.rem(unit, HALF)
            tile = own + at
            b_copy(group, tile, near, 0).wait_recv()
            total = part[group, tile].astype(F32) + chain[group, tile].astype(F32)

            @pl.when(unit < BACKS)
            def _():
                part[group, tile] = total.astype(BF)

            @pl.when(unit >= BACKS)
            def _():
                head = group - 2
                columns = pl.ds(pl.multiple_of(lax.rem(head, 3) * HEAD, HEAD), HEAD)
                found[head, tile] = attend(total, part[head // 3, tile, :, columns], mask[at])

            later = unit + AHEAD

            @pl.when((later >= BACKS) & (later < SUMS))
            def _():
                project(later)

            @pl.when(later < SUMS)
            def _():
                b_free(later)
                b_out(later).start()

            @pl.when(later >= SUMS + SLOTS)
            def _():
                c_free(later - SUMS)

            @pl.when(later >= SUMS)
            def _():
                c_out(later - SUMS).start()

        run(send_out, 0, SLOTS)
        take_tiles()
        run(send_out, SLOTS, AHEAD)
        make_masks()
        run(finish, 0, BACKS - AHEAD)
        take_quarters()
        run(finish, BACKS - AHEAD, SUMS)

    @pl.when(is_mid)
    def _():
        def add_on(unit, base, to, stream):
            group = unit // HALF
            tile = base + lax.rem(unit, HALF)
            b_copy(group, tile, to, 0).wait_recv()
            part[group, tile] = (
                part[group, tile].astype(F32) + chain[group, tile].astype(F32)
            ).astype(BF)

            @pl.when(unit >= SLOTS)
            def _():
                b_free(unit, stream)

            b_copy(group, tile, to, slot_of(unit, stream)).start()

        def pass_on(unit):
            @pl.when(unit < SUMS)
            def _():
                add_on(unit, far_base, middle, 0)

            @pl.when(unit >= LAG)
            def _():
                add_on(unit - LAG, edge_base, edge, 1)

            @pl.when((unit >= BACKS) & (unit + HALF < SUMS))
            def _():
                project(unit + HALF)

        run(project_back, 0, BACKS)
        take_tiles()
        run(pass_on, 0, BACKS)
        take_quarters()
        run(project, BACKS, BACKS + HALF)
        run(pass_on, BACKS, SUMS + LAG)
        for step in range(1, LOADERS):
            i_copy(step).wait_recv()

    feat_acc[...] = jnp.zeros_like(feat_acc)

    def core_copy(chunk):
        return remote(
            grads.at[chunk, :, 1 - core], core_in.at[chunk],
            core_send.at[chunk], core_recv.at[chunk], core_peer,
        )

    def y_copy(chunk, step):
        return remote(
            core_sum.at[chunk, pl.ds(2 * lax.rem(row + step, 4), 2)], y_in.at[chunk, step - 1],
            y_send.at[chunk, step - 1], y_recv.at[chunk, step - 1], row_peer(step),
        )

    def z_copy(chunk):
        return remote(
            y_sum.at[chunk, 1 - high], z_in.at[chunk],
            z_send.at[chunk], z_recv.at[chunk], high_peer,
        )

    def stage_core(chunk):
        core_copy(chunk).wait_recv()
        core_sum[chunk] = (
            grads[chunk, :, core].astype(F32) + core_in[chunk].astype(F32)
        ).astype(BF)
        for step in (2, 1, 3):
            y_copy(chunk, step).start()

    def stage_row(chunk):
        total = core_sum[chunk, pl.ds(2 * row, 2)].astype(F32)
        for step in (1, 3, 2):
            y_copy(chunk, step).wait_recv()
            total = total + y_in[chunk, step - 1].astype(F32)
        y_sum[chunk] = total.astype(BF)
        z_copy(chunk).start()

    def stage_high(chunk):
        z_copy(chunk).wait_recv()
        return (y_sum[chunk, high].astype(F32) + z_in[chunk].astype(F32)) * (1.0 / 16.0)

    def store_qkv(chunk):
        columns = pl.ds(pl.multiple_of(chunk * QKV, HEAD), QKV)
        out_qkv[0, :, columns] = stage_high(chunk)

    def hand_on(unit, base, to, stream):
        head = unit // HALF
        tile = base + lax.rem(unit, HALF)
        c_copy(head, tile, to, 0).wait_recv()

        @pl.when(unit >= SLOTS)
        def _():
            c_free(unit, stream)

        c_copy(head, tile, to, slot_of(unit, stream)).start()

    def weight_step(unit, carry):
        @pl.when(is_mid)
        def _():
            @pl.when(unit < UNITS)
            def _():
                hand_on(unit, edge_base, middle, 0)

            @pl.when((unit >= LAG) & (unit < UNITS + LAG))
            def _():
                hand_on(unit - LAG, far_base, edge, 1)

        @pl.when(is_end)
        def _():
            @pl.when(unit + AHEAD < UNITS)
            def _():
                c_free(unit + AHEAD)
                c_out(unit + AHEAD).start()

            @pl.when((unit >= LAG) & (unit < UNITS + LAG))
            def _():
                got = unit - LAG
                c_copy(got // HALF, other + lax.rem(got, HALF), near, 0).wait_recv()

        @pl.when(unit < HALF)
        def _():
            for tile in range(2):
                columns = pl.ds(pl.multiple_of((2 * unit + tile) * PATCH, PATCH), PATCH)
                feat_t[:, columns] = feat[2 * unit + tile].T

        @pl.when(unit >= HALF - 1 + LAG)
        def _():
            done = unit - (HALF - 1 + LAG)
            head = done // HALF
            at = lax.rem(done, HALF)
            grad = found[head, :, :, HEAD:].reshape(TILES * PATCH, QKV)
            lines = pl.ds(pl.multiple_of(at * 192, 64), 192)
            piece = dot(feat_t[lines, :], grad, NN).astype(BF)
            grads[head, pl.ds(2 * at, 2)] = piece.reshape(2, 2, 48, QKV)
            tiles = pl.ds(2 * at, 2)
            columns = pl.ds(pl.multiple_of(head * QKV, HEAD), QKV)
            back = dot(
                found[head, tiles, :, HEAD:].reshape(2 * PATCH, QKV), w_qkv[:, columns], NT
            )
            feat_acc[tiles] += back.reshape(2, PATCH, WIDE)

            @pl.when(at == 0)
            def _():
                lines = pl.ds(pl.multiple_of(head * HEAD, HEAD), HEAD)
                grad_wide[lines, :] = dot(
                    found[head, :, :, :HEAD].reshape(TILES * PATCH, HEAD),
                    cot[...].reshape(TILES * PATCH, WIDE),
                    TN,
                ).astype(BF)

            @pl.when((at == 1) & (head >= 1))
            def _():
                stage_core(head - 1)

            @pl.when((at == 2) & (head >= 2))
            def _():
                stage_row(head - 2)

            @pl.when((at == 3) & (head >= 3))
            def _():
                store_qkv(head - 3)

            @pl.when(at == 3)
            def _():
                core_copy(head).start()

        return carry

    lax.fori_loop(0, UNITS + HALF - 1 + LAG, weight_step, 0)

    for half in range(2):
        columns = slice(half * QKV, (half + 1) * QKV)
        grads[6 + half] = grad_wide[:, columns].reshape(8, 2, 48, QKV)
        core_copy(6 + half).start()

    def d_copy(step):
        lines = pl.ds(pl.multiple_of(lax.rem(my + step, 4) * 32, 32), 32)
        return remote(
            feat_bf.at[:, lines], feat_in.at[step - 1],
            d_send.at[step - 1], d_recv.at[step - 1], x_peer(step),
        )

    feat_bf[...] = feat_acc[...].astype(BF)
    for step in (2, 1, 3):
        d_copy(step).start()
    stage_core(5)
    stage_row(4)
    stage_core(6)
    stage_core(7)
    stage_row(5)
    store_qkv(3)
    store_qkv(4)
    stage_row(6)
    stage_row(7)
    store_qkv(5)
    total = feat_acc[:, mine, :]
    for step in (1, 3, 2):
        d_copy(step).wait_recv()
        total = total + feat_in[step - 1].astype(F32)
    out_feat[...] = total.astype(BF)
    out_out[0, :, :QKV] = stage_high(6)
    out_out[0, :, QKV:] = stage_high(7)

    for step in range(1, LOADERS):
        a_copy(step).wait_send()
        i_copy(step).wait_send()
    for step in range(1, 4):
        x_copy(step).wait_send()
        d_copy(step).wait_send()

    def drain(chunk, carry):
        core_copy(chunk).wait_send()
        z_copy(chunk).wait_send()
        for step in range(1, 4):
            y_copy(chunk, step).wait_send()
        return carry

    lax.fori_loop(0, CHUNKS, drain, 0)

    for slot in range(SLOTS):
        b_free(slot)
        c_free(slot)

    @pl.when(is_mid)
    def _():
        for slot in range(SLOTS):
            b_free(slot, 1)
            c_free(slot, 1)


def shards(features, segment_ids, owners, w_qkv, w_out, cotangent):
    vmem = pl.BlockSpec(memory_space=pltpu.VMEM)
    smem = pl.BlockSpec(memory_space=pltpu.SMEM)
    dma = pltpu.SemaphoreType.DMA
    units = (HEADS_HERE, TILES, PATCH, UNIT)
    sums = (GROUPS, TILES, PATCH, QKV)
    return pl.pallas_call(
        branch,
        out_shape=(
            jax.ShapeDtypeStruct((TILES, 32, WIDE), BF),
            jax.ShapeDtypeStruct((1, 48, HEADS_HERE * QKV), F32),
            jax.ShapeDtypeStruct((1, 48, WIDE), F32),
        ),
        in_specs=[smem] + [vmem] * 5,
        out_specs=(vmem,) * 3,
        scratch_shapes=[
            pltpu.VMEM((TILES, PATCH, WIDE), BF),
            pltpu.VMEM((WIDE, TILES * PATCH), BF),
            pltpu.VMEM(sums, BF),
            pltpu.VMEM(sums, BF),
            pltpu.VMEM(units, BF),
            pltpu.VMEM((CHUNKS, 8, 2, 48, QKV), BF),
            pltpu.VMEM((CHUNKS, 8, 48, QKV), BF),
            pltpu.VMEM((CHUNKS, 8, 48, QKV), BF),
            pltpu.VMEM((CHUNKS, 3, 2, 48, QKV), BF),
            pltpu.VMEM((CHUNKS, 2, 48, QKV), BF),
            pltpu.VMEM((CHUNKS, 48, QKV), BF),
            pltpu.VMEM((WIDE, WIDE), BF),
            pltpu.VMEM((TILES, PATCH, WIDE), F32),
            pltpu.VMEM((TILES, PATCH, WIDE), BF),
            pltpu.VMEM((3, TILES, QUARTER, WIDE), BF),
            pltpu.VMEM((LOADERS, QUARTER, WIDE), BF),
            pltpu.VMEM((LOADERS, QUARTER, WIDE), BF),
            pltpu.VMEM((LOADERS, TILES, PATCH), jnp.int32),
            pltpu.VMEM((HALF, PATCH, PATCH), F32),
            dma((LOADERS - 1,)), dma((LOADERS - 1,)),
            dma((LOADERS - 1,)), dma((LOADERS - 1,)),
            dma((3,)), dma((3,)),
            dma((2 * SLOTS,)), dma((GROUPS, TILES)),
            dma((2 * SLOTS,)), dma((HEADS_HERE, TILES)),
            dma((CHUNKS,)), dma((CHUNKS,)),
            dma((CHUNKS, 3)), dma((CHUNKS, 3)),
            dma((CHUNKS,)), dma((CHUNKS,)),
            dma((3,)), dma((3,)),
        ],
        compiler_params=pltpu.CompilerParams(
            collective_id=0, has_side_effects=True, vmem_limit_bytes=60 * 1024 * 1024
        ),
        cost_estimate=pl.CostEstimate(
            flops=14_000_000_000, bytes_accessed=12_000_000, transcendentals=400_000
        ),
    )(owners, features, segment_ids, cotangent, w_qkv, w_out)


def solution(mesh):
    return jax.shard_map(
        shards,
        mesh=mesh,
        in_specs=(
            P("dp", None, "mx"),
            P("dp", None),
            P(),
            P("mx", "my"),
            P("my", "mx"),
            P("dp", None, "mx"),
        ),
        out_specs=(P("dp", "my", "mx"), P("mx", "dp", "my"), P("my", "dp", "mx")),
        check_vma=False,
    )
```

```python
import jax
import jax.numpy as jnp
from jax import lax
from jax.experimental import pallas as pl
from jax.experimental.pallas import tpu as pltpu
from jax.sharding import PartitionSpec as P

HEAD = 128
HEADS_HERE = 6
TILES = 8
HALF = 4
GROUPS = HEADS_HERE + 2
BACKS = 2 * HALF
LOADERS = 16
QUARTER = 32
PATCH = 128
WIDE = 768
QKV = 3 * HEAD
UNIT = QKV + HEAD
CHUNKS = 8
SLOTS = ((0, 0), (0, 1), (-1, 0), (-2, 0), (1, 0), (1, 1), (2, 1), (-1, 1))
SUM_SENDS = ((4, True), (5, True), (6, True), (2, False), (3, False), (7, False))
ROW_SENDS = (
    (0, 2, True), (1, 7, True), (2, 3, True), (0, 4, False), (1, 5, False), (5, 6, False)
)
BF = jnp.bfloat16
F32 = jnp.float32
MESH = pl.DeviceIdType.MESH
SCALE = HEAD ** (-0.5)


def dot(a, b, contract):
    return lax.dot_general(a, b, ((contract[0], contract[1]), ((), ())), preferred_element_type=F32)


NN = ((1,), (0,))
NT = ((1,), (1,))
TN = ((0,), (0,))


def normalize(values):
    centered = values - jnp.mean(values, axis=-1, keepdims=True)
    inverse = lax.rsqrt(jnp.mean(centered * centered, axis=-1, keepdims=True) + 1e-06)
    return centered * inverse, inverse


def norm_back(grad_hat, normed, inverse):
    return inverse * (
        grad_hat
        - jnp.mean(grad_hat, axis=-1, keepdims=True)
        - normed * jnp.mean(grad_hat * normed, axis=-1, keepdims=True)
    )


def attend(total, grad_bf, mask):
    query_hat, query_inv = normalize(total[:, :HEAD])
    key_hat, key_inv = normalize(total[:, HEAD : 2 * HEAD])
    query_bf = query_hat.astype(BF)
    key_bf = key_hat.astype(BF)
    value_bf = total[:, 2 * HEAD :].astype(BF)
    expo = jnp.exp(dot(query_bf, key_bf, NT) * SCALE) * mask
    weights = expo / jnp.sum(expo, axis=-1, keepdims=True)
    weights_bf = weights.astype(BF)
    attended = dot(weights_bf, value_bf, NN)
    grad_value = dot(weights_bf, grad_bf, TN)
    grad_weights = dot(grad_bf, value_bf, NT)
    grad_scores = (
        weights
        * (grad_weights - jnp.sum(weights * grad_weights, axis=-1, keepdims=True))
        * SCALE
    ).astype(BF)
    grad_query = norm_back(dot(grad_scores, key_bf, NN), query_hat, query_inv)
    grad_key = norm_back(dot(grad_scores, query_bf, TN), key_hat, key_inv)
    return jnp.concatenate([attended, grad_query, grad_key, grad_value], axis=1).astype(BF)


def branch(
    owners, given, given_ids, cot_given, w_qkv, w_out,
    out_feat, out_qkv, out_out,
    feat, cot, feat_t, part, chain, found, grads, core_in, core_sum, y_in, y_sum, z_in,
    grad_wide, feat_acc, feat_bf, feat_in, outbox, inbox, ids, mask,
    stage, back_out, back_in, cross_send, cross_recv, spread_send, spread_recv,
    a_send, a_recv, i_send, i_recv, b_send, b_recv, c_send, c_recv,
    core_send, core_recv, y_send, y_recv, z_send, z_recv, d_send, d_recv,
):
    dp = lax.axis_index("dp")
    mx = lax.axis_index("mx")
    my = lax.axis_index("my")
    core = lax.rem(dp, 2)
    high = lax.rem(dp // 2, 2)
    row = dp // 4
    core_peer = (dp + 1 - 2 * core, mx, my)
    high_peer = (row * 4 + (1 - high) * 2 + core, mx, my)

    def row_peer(step):
        return (lax.rem(row + step, 4) * 4 + lax.rem(dp, 4), mx, my)

    def x_peer(step):
        return (dp, mx, lax.rem(my + step, 4))

    turned = row * 4 + (1 - high) * 2 + core
    right = (jnp.where(mx == 3, turned, dp), lax.rem(mx + 1, 4), my)
    left = (jnp.where(mx == 0, turned, dp), lax.rem(mx + 3, 4), my)

    barrier = pltpu.get_barrier_semaphore()

    def greet(peer):
        pl.semaphore_signal(barrier, inc=1, device_id=peer, device_id_type=MESH)

    def dp_peer(step):
        return (lax.rem(dp + step, LOADERS), mx, my)

    for step in range(1, LOADERS):
        greet(dp_peer(step))
    for step in range(1, 4):
        greet(x_peer(step))

    greet(right)
    greet(left)
    pl.semaphore_wait(barrier, 20)

    def remote(src, dst, send, recv, peer):
        return pltpu.make_async_remote_copy(
            src_ref=src, dst_ref=dst, send_sem=send, recv_sem=recv,
            device_id=peer, device_id_type=MESH,
        )

    mine = pl.ds(pl.multiple_of(my * QUARTER, QUARTER), QUARTER)

    def tile_of(slot):
        ahead, which = SLOTS[slot]
        return 2 * lax.rem(mx + ahead + 4, 4) + which

    def crosses(slot):
        ahead = SLOTS[slot][0]
        return (mx + ahead < 0) | (mx + ahead > 3)

    def cross_copy(kind, slot):
        src = (cot_given.at[tile_of(slot), mine], stage.at[slot], back_out.at[slot])[kind]
        dst = (cot.at[slot, mine], feat.at[slot, mine], back_in.at[slot])[kind]
        return remote(
            src, dst, cross_send.at[kind, slot], cross_recv.at[kind, slot], high_peer
        )

    def spread_copy(kind, slot, step):
        held = (cot, feat)[kind].at[slot, mine]
        return remote(
            held, held, spread_send.at[kind, slot, step - 1],
            spread_recv.at[kind, slot, step - 1], x_peer(step),
        )

    def spread(kind, slot):
        for step in (2, 1, 3):
            spread_copy(kind, slot, step).start()

    def gather(kind, slot):
        for step in (1, 3, 2):
            spread_copy(kind, slot, step).wait_recv()

    for slot in range(2, TILES):
        @pl.when(crosses(slot))
        def _():
            cross_copy(0, slot).start()

    def position(loader, owner):
        place = jnp.int32(0)
        for tile in range(TILES):
            place = jnp.where(owners[loader, tile] == owner, tile, place)
        return place

    def fill(owner, carry):
        outbox[owner] = given[position(dp, owner), mine, :]
        return carry

    lax.fori_loop(0, LOADERS, fill, 0)

    def a_copy(step):
        return remote(
            outbox.at[lax.rem(dp + step, LOADERS)], inbox.at[dp],
            a_send.at[step - 1], a_recv.at[step - 1], dp_peer(step),
        )

    def i_copy(step):
        return remote(
            given_ids, ids.at[dp], i_send.at[step - 1], i_recv.at[step - 1], dp_peer(step)
        )

    for step in (2, 6, 10, 14, 1, 3, 5, 7, 9, 11, 13, 15, 4, 12, 8):
        a_copy(step).start()
        i_copy(step).start()
    inbox[dp] = outbox[dp]
    ids[dp] = given_ids[...]

    loaders = [jnp.int32(0)] * TILES
    places = [jnp.int32(0)] * TILES
    count = jnp.int32(0)
    for loader in range(LOADERS):
        here = jnp.int32(0)
        for tile in range(TILES):
            here = jnp.where(owners[loader, tile] == dp, 1, here)
        place = position(loader, dp)
        for tile in range(TILES):
            fits = (here > 0) & (count == tile)
            loaders[tile] = jnp.where(fits, loader, loaders[tile])
            places[tile] = jnp.where(fits, place, places[tile])
        count = count + here

    for slot in range(TILES):
        @pl.when(jnp.logical_not(crosses(slot)))
        def _():
            cot[slot] = cot_given[tile_of(slot)]

    def by_place(values, ahead, which):
        found_value = values[which]
        for place in range(4):
            found_value = jnp.where(
                lax.rem(mx + ahead + 4, 4) == place, values[2 * place + which], found_value
            )
        return found_value

    def take_tiles():
        for step in range(1, LOADERS):
            a_copy(step).wait_recv()
        for slot in (2, 3, 4, 5, 6, 7, 0, 1):
            loader = by_place(loaders, *SLOTS[slot])

            @pl.when(crosses(slot))
            def _():
                stage[slot] = inbox[loader]
                cross_copy(1, slot).start()

            @pl.when(jnp.logical_not(crosses(slot)))
            def _():
                feat[slot, mine, :] = inbox[loader]
                spread(1, slot)

    def make_masks():
        for step in range(1, LOADERS):
            i_copy(step).wait_recv()
        for tile in range(2):
            loader = by_place(loaders, 0, tile)
            place = by_place(places, 0, tile)
            line = ids[loader, pl.ds(place, 1), :].astype(F32)
            across = jnp.broadcast_to(line, (PATCH, PATCH))
            mask[tile] = (across == across.T).astype(F32)

    def project_back(unit):
        half = unit // HALF
        tile = lax.rem(unit, HALF)
        rows = jnp.concatenate([cot[tile], cot[tile + HALF]], axis=0)
        lines = pl.ds(pl.multiple_of(half * QKV, HEAD), QKV)
        product = dot(rows, w_out[lines, :], NT).astype(BF)
        part[half, tile] = product[:PATCH]
        part[half, tile + HALF] = product[PATCH:]

    def project(unit):
        group = unit // HALF
        tile = lax.rem(unit, HALF)
        rows = jnp.concatenate([feat[tile], feat[tile + HALF]], axis=0)
        columns = pl.ds(pl.multiple_of((group - 2) * QKV, HEAD), QKV)
        product = dot(rows, w_qkv[:, columns], NN).astype(BF)
        part[group, tile] = product[:PATCH]
        part[group, tile + HALF] = product[PATCH:]

    def run(function, start, stop):
        def step(unit, carry):
            function(unit)
            return carry

        lax.fori_loop(start, stop, step, 0)

    def b_copy(group, which):
        slot, to_right = SUM_SENDS[which]
        return remote(
            part.at[group, slot], chain.at[group, which],
            b_send.at[group, which], b_recv.at[group, which], right if to_right else left,
        )

    def c_copy(head, which):
        slot, there, to_right = ROW_SENDS[which]
        return remote(
            found.at[head, slot], found.at[head, there],
            c_send.at[head, which], c_recv.at[head, which], right if to_right else left,
        )

    def b_first(group):
        for which in (2, 4, 0, 5):
            b_copy(group, which).start()

    def b_forward(group):
        for come, slot, go in ((2, 5, 1), (4, 2, 3)):
            b_copy(group, come).wait_recv()
            part[group, slot] = (
                part[group, slot].astype(F32) + chain[group, come].astype(F32)
            ).astype(BF)
            b_copy(group, go).start()

    def b_total(group, tile):
        total = part[group, tile].astype(F32)
        for come in ((0, 3), (1, 5))[tile]:
            b_copy(group, come).wait_recv()
            total = total + chain[group, come].astype(F32)
        return total

    def c_first(head):
        for which in (0, 4, 3, 1):
            c_copy(head, which).start()

    def c_forward(head):
        for come, go in ((0, 2), (4, 5)):
            c_copy(head, come).wait_recv()
            c_copy(head, go).start()

    def c_finish(head):
        for which in (1, 2, 3, 5):
            c_copy(head, which).wait_recv()

    def attend_head(head):
        columns = pl.ds(pl.multiple_of(lax.rem(head, 3) * HEAD, HEAD), HEAD)
        totals = [b_total(head + 2, tile) for tile in range(2)]
        for tile in range(2):
            found[head, tile] = attend(
                totals[tile], part[head // 3, tile, :, columns], mask[tile]
            )
        c_first(head)

    for slot in range(2, TILES):
        @pl.when(crosses(slot))
        def _():
            cross_copy(0, slot).wait_recv()
            spread(0, slot)

    for slot in range(2, TILES):
        @pl.when(crosses(slot))
        def _():
            gather(0, slot)

    run(project_back, 0, BACKS)
    for group in range(2):
        b_first(group)
    take_tiles()
    for slot in range(2, TILES):
        @pl.when(crosses(slot))
        def _():
            cross_copy(1, slot).wait_recv()
            spread(1, slot)

    make_masks()
    for group in range(2):
        b_forward(group)
    for slot in range(TILES):
        gather(1, slot)
    run(project, BACKS, BACKS + HALF)
    b_first(2)
    for group in range(2):
        for tile in range(2):
            part[group, tile] = b_total(group, tile).astype(BF)

    feat_acc[...] = jnp.zeros_like(feat_acc)

    def core_copy(chunk):
        return remote(
            grads.at[chunk, :, 1 - core], core_in.at[chunk],
            core_send.at[chunk], core_recv.at[chunk], core_peer,
        )

    def y_copy(chunk, step):
        return remote(
            core_sum.at[chunk, pl.ds(2 * lax.rem(row + step, 4), 2)], y_in.at[chunk, step - 1],
            y_send.at[chunk, step - 1], y_recv.at[chunk, step - 1], row_peer(step),
        )

    def z_copy(chunk):
        return remote(
            y_sum.at[chunk, 1 - high], z_in.at[chunk],
            z_send.at[chunk], z_recv.at[chunk], high_peer,
        )

    def stage_core(chunk):
        core_copy(chunk).wait_recv()
        core_sum[chunk] = (
            grads[chunk, :, core].astype(F32) + core_in[chunk].astype(F32)
        ).astype(BF)
        for step in (2, 1, 3):
            y_copy(chunk, step).start()

    def stage_row(chunk):
        total = core_sum[chunk, pl.ds(2 * row, 2)].astype(F32)
        for step in (1, 3, 2):
            y_copy(chunk, step).wait_recv()
            total = total + y_in[chunk, step - 1].astype(F32)
        y_sum[chunk] = total.astype(BF)
        z_copy(chunk).start()

    def stage_high(chunk):
        z_copy(chunk).wait_recv()
        return (y_sum[chunk, high].astype(F32) + z_in[chunk].astype(F32)) * (1.0 / 16.0)

    def store_qkv(chunk):
        columns = pl.ds(pl.multiple_of(chunk * QKV, HEAD), QKV)
        out_qkv[0, :, columns] = stage_high(chunk)

    def weight_piece(head, at):
        grad = found[head, :, :, HEAD:].reshape(TILES * PATCH, QKV)
        lines = pl.ds(pl.multiple_of(at * 192, 64), 192)
        piece = dot(feat_t[lines, :], grad, NN).astype(BF)
        grads[head, pl.ds(2 * at, 2)] = piece.reshape(2, 2, 48, QKV)
        tiles = pl.ds(2 * at, 2)
        columns = pl.ds(pl.multiple_of(head * QKV, HEAD), QKV)
        back = dot(found[head, tiles, :, HEAD:].reshape(2 * PATCH, QKV), w_qkv[:, columns], NT)
        feat_acc[tiles] += back.reshape(2, PATCH, WIDE)

    def weights(head):
        run(lambda at: weight_piece(head, at), 0, 4)
        core_copy(head).start()
        lines = pl.ds(pl.multiple_of(head * HEAD, HEAD), HEAD)
        grad_wide[lines, :] = dot(
            found[head, :, :, :HEAD].reshape(TILES * PATCH, HEAD),
            cot[...].reshape(TILES * PATCH, WIDE),
            TN,
        ).astype(BF)

    def when(least, head, function):
        @pl.when((head >= least) & (head < HEADS_HERE))
        def _():
            function(head)

    def head_step(now):
        when(1, now, lambda head: b_first(head + 2))
        when(0, now - 1, lambda head: b_forward(head + 2))
        when(0, now - 3, c_forward)
        when(1, now + 1, lambda head: run(project, BACKS + HALF * head, BACKS + HALF * head + HALF))
        when(0, now - 2, attend_head)

        @pl.when(now < 4)
        def _():
            for tile in range(2):
                columns = pl.ds(pl.multiple_of((2 * now + tile) * PATCH, PATCH), PATCH)
                feat_t[:, columns] = feat[2 * now + tile].T

        when(0, now - 4, c_finish)
        when(0, now - 4, weights)

        @pl.when(now >= 5)
        def _():
            stage_core(now - 5)

        @pl.when(now >= 6)
        def _():
            stage_row(now - 6)

        @pl.when(now >= 7)
        def _():
            store_qkv(now - 7)

    run(head_step, 0, HEADS_HERE + 4)

    for half in range(2):
        columns = slice(half * QKV, (half + 1) * QKV)
        grads[6 + half] = grad_wide[:, columns].reshape(8, 2, 48, QKV)
        core_copy(6 + half).start()

    def d_copy(step):
        lines = pl.ds(pl.multiple_of(lax.rem(my + step, 4) * 32, 32), 32)
        return remote(
            feat_bf.at[:, lines], feat_in.at[step - 1],
            d_send.at[step - 1], d_recv.at[step - 1], x_peer(step),
        )

    feat_bf[...] = feat_acc[...].astype(BF)
    for step in (2, 1, 3):
        d_copy(step).start()
    stage_core(5)
    stage_row(4)
    stage_core(6)
    stage_core(7)
    stage_row(5)
    store_qkv(3)
    store_qkv(4)
    stage_row(6)
    for step in (1, 3, 2):
        d_copy(step).wait_recv()
    for slot in (2, 3, 4, 5, 6, 7, 0, 1):
        total = feat_acc[slot, mine, :]
        for step in (1, 3, 2):
            total = total + feat_in[step - 1, slot].astype(F32)
        total = total.astype(BF)

        @pl.when(crosses(slot))
        def _():
            back_out[slot] = total
            cross_copy(2, slot).start()

        @pl.when(jnp.logical_not(crosses(slot)))
        def _():
            out_feat[tile_of(slot)] = total

    stage_row(7)
    store_qkv(5)
    out_out[0, :, :QKV] = stage_high(6)
    out_out[0, :, QKV:] = stage_high(7)
    for slot in range(2, TILES):
        @pl.when(crosses(slot))
        def _():
            cross_copy(2, slot).wait_recv()
            out_feat[tile_of(slot)] = back_in[slot]

    for step in range(1, LOADERS):
        a_copy(step).wait_send()
        i_copy(step).wait_send()
    for step in range(1, 4):
        d_copy(step).wait_send()
    for slot in range(TILES):
        @pl.when(crosses(slot))
        def _():
            for kind in range(3):
                cross_copy(kind, slot).wait_send()
            for step in range(1, 4):
                spread_copy(0, slot, step).wait_send()

        for step in range(1, 4):
            spread_copy(1, slot, step).wait_send()

    def drain(chunk, carry):
        core_copy(chunk).wait_send()
        z_copy(chunk).wait_send()
        for step in range(1, 4):
            y_copy(chunk, step).wait_send()
        return carry

    lax.fori_loop(0, CHUNKS, drain, 0)

    def drain_group(group):
        for which in range(6):
            b_copy(group, which).wait_send()

    def drain_head(head):
        for which in range(6):
            c_copy(head, which).wait_send()

    run(drain_group, 0, GROUPS)
    run(drain_head, 0, HEADS_HERE)


def shards(features, segment_ids, owners, w_qkv, w_out, cotangent):
    vmem = pl.BlockSpec(memory_space=pltpu.VMEM)
    smem = pl.BlockSpec(memory_space=pltpu.SMEM)
    dma = pltpu.SemaphoreType.DMA
    units = (HEADS_HERE, TILES, PATCH, UNIT)
    sums = (GROUPS, TILES, PATCH, QKV)
    return pl.pallas_call(
        branch,
        out_shape=(
            jax.ShapeDtypeStruct((TILES, 32, WIDE), BF),
            jax.ShapeDtypeStruct((1, 48, HEADS_HERE * QKV), F32),
            jax.ShapeDtypeStruct((1, 48, WIDE), F32),
        ),
        in_specs=[smem] + [vmem] * 5,
        out_specs=(vmem,) * 3,
        scratch_shapes=[
            pltpu.VMEM((TILES, PATCH, WIDE), BF),
            pltpu.VMEM((TILES, PATCH, WIDE), BF),
            pltpu.VMEM((WIDE, TILES * PATCH), BF),
            pltpu.VMEM(sums, BF),
            pltpu.VMEM((GROUPS, 6, PATCH, QKV), BF),
            pltpu.VMEM(units, BF),
            pltpu.VMEM((CHUNKS, 8, 2, 48, QKV), BF),
            pltpu.VMEM((CHUNKS, 8, 48, QKV), BF),
            pltpu.VMEM((CHUNKS, 8, 48, QKV), BF),
            pltpu.VMEM((CHUNKS, 3, 2, 48, QKV), BF),
            pltpu.VMEM((CHUNKS, 2, 48, QKV), BF),
            pltpu.VMEM((CHUNKS, 48, QKV), BF),
            pltpu.VMEM((WIDE, WIDE), BF),
            pltpu.VMEM((TILES, PATCH, WIDE), F32),
            pltpu.VMEM((TILES, PATCH, WIDE), BF),
            pltpu.VMEM((3, TILES, QUARTER, WIDE), BF),
            pltpu.VMEM((LOADERS, QUARTER, WIDE), BF),
            pltpu.VMEM((LOADERS, QUARTER, WIDE), BF),
            pltpu.VMEM((LOADERS, TILES, PATCH), jnp.int32),
            pltpu.VMEM((2, PATCH, PATCH), F32),
            pltpu.VMEM((TILES, QUARTER, WIDE), BF),
            pltpu.VMEM((TILES, QUARTER, WIDE), BF),
            pltpu.VMEM((TILES, QUARTER, WIDE), BF),
            dma((3, TILES)), dma((3, TILES)),
            dma((2, TILES, 3)), dma((2, TILES, 3)),
            dma((LOADERS - 1,)), dma((LOADERS - 1,)),
            dma((LOADERS - 1,)), dma((LOADERS - 1,)),
            dma((GROUPS, 6)), dma((GROUPS, 6)),
            dma((HEADS_HERE, 6)), dma((HEADS_HERE, 6)),
            dma((CHUNKS,)), dma((CHUNKS,)),
            dma((CHUNKS, 3)), dma((CHUNKS, 3)),
            dma((CHUNKS,)), dma((CHUNKS,)),
            dma((3,)), dma((3,)),
        ],
        compiler_params=pltpu.CompilerParams(
            collective_id=0, has_side_effects=True, vmem_limit_bytes=60 * 1024 * 1024
        ),
        cost_estimate=pl.CostEstimate(
            flops=14_000_000_000, bytes_accessed=12_000_000, transcendentals=400_000
        ),
    )(owners, features, segment_ids, cotangent, w_qkv, w_out)


def solution(mesh):
    return jax.shard_map(
        shards,
        mesh=mesh,
        in_specs=(
            P("dp", None, "mx"),
            P("dp", None),
            P(),
            P("mx", "my"),
            P("my", "mx"),
            P("dp", None, "mx"),
        ),
        out_specs=(P("dp", "my", "mx"), P("mx", "dp", "my"), P("my", "dp", "mx")),
        check_vma=False,
    )
```

```python
import jax
import jax.numpy as jnp
from jax import lax
from jax.experimental import pallas as pl
from jax.experimental.pallas import tpu as pltpu
from jax.sharding import PartitionSpec as P

HEAD = 128
HEADS_HERE = 6
TILES = 8
HALF = 2
HELD = 4
BOTH = 2 * 768
PIECE = 96
GROUPS = HEADS_HERE + 2
BACKS = 2 * HALF
LOADERS = 16
QUARTER = 32
PATCH = 128
WIDE = 768
QKV = 3 * HEAD
UNIT = QKV + HEAD
CHUNKS = HEADS_HERE
HALF_ROWS = 384
SLOTS = ((0, 0), (0, 1), (-1, 0), (1, 1))


def routes():
    table = {}
    for block in range(4):
        for place in range(4):
            for which in range(2):
                off = 0 if (place - block) % 2 == 0 else 1 - 2 * which
                to = place + off
                slot = which if off == 0 else 2 + which
                table.setdefault((slot, int(to % 4 != block)), {})[block] = (
                    2 * place + which, int(not 0 <= to <= 3)
                )
    return table


ROUTES = routes()
MOVED = tuple((slot, block) for block in (1, 0) for slot in range(4))
WAVES = 2
WAVE = WIDE // WAVES
BF = jnp.bfloat16
F32 = jnp.float32
MESH = pl.DeviceIdType.MESH
SCALE = HEAD ** (-0.5)


def dot(a, b, contract):
    return lax.dot_general(a, b, ((contract[0], contract[1]), ((), ())), preferred_element_type=F32)


NN = ((1,), (0,))
NT = ((1,), (1,))
TN = ((0,), (0,))


def normalize(values):
    centered = values - jnp.mean(values, axis=-1, keepdims=True)
    inverse = lax.rsqrt(jnp.mean(centered * centered, axis=-1, keepdims=True) + 1e-06)
    return centered * inverse, inverse


def norm_back(grad_hat, normed, inverse):
    return inverse * (
        grad_hat
        - jnp.mean(grad_hat, axis=-1, keepdims=True)
        - normed * jnp.mean(grad_hat * normed, axis=-1, keepdims=True)
    )


def attend(total, grad_bf, mask):
    query_hat, query_inv = normalize(total[:, :HEAD])
    key_hat, key_inv = normalize(total[:, HEAD : 2 * HEAD])
    query_bf = query_hat.astype(BF)
    key_bf = key_hat.astype(BF)
    value_bf = total[:, 2 * HEAD :].astype(BF)
    expo = jnp.exp(dot(query_bf, key_bf, NT) * SCALE) * mask
    weights = expo / jnp.sum(expo, axis=-1, keepdims=True)
    weights_bf = weights.astype(BF)
    attended = dot(weights_bf, value_bf, NN)
    grad_value = dot(weights_bf, grad_bf, TN)
    grad_weights = dot(grad_bf, value_bf, NT)
    grad_scores = (
        weights
        * (grad_weights - jnp.sum(weights * grad_weights, axis=-1, keepdims=True))
        * SCALE
    ).astype(BF)
    grad_query = norm_back(dot(grad_scores, key_bf, NN), query_hat, query_inv)
    grad_key = norm_back(dot(grad_scores, query_bf, TN), key_hat, key_inv)
    return jnp.concatenate([attended, grad_query, grad_key, grad_value], axis=1).astype(BF)


def branch(
    owners, features, given_ids, cot_given, w_qkv_given, w_out_given,
    out_feat, out_qkv, out_out,
    given, w_qkv, w_out, load_sem, feat, cot, feat_t, part, chain, found, grads, core_in, core_sum, y_in, y_sum, z_in,
    half_grad, half_in, half_sum, half_y, half_ysum, half_z, grad_wide, feat_acc, feat_bf, feat_in, outbox, inbox_first, inbox_second, ids, mask,
    w_far_send, w_far_recv, w_row_send, w_row_recv, w_core_send, w_core_recv,
    stage, back_out, back_in, cross_send, cross_recv, spread_send, spread_recv,
    a_send, a_recv, i_send, i_recv, b_send, b_recv, c_send, c_recv,
    half_core_send, half_core_recv, half_row_send, half_row_recv, half_high_send, half_high_recv,
    core_send, core_recv, y_send, y_recv, z_send, z_recv, d_send, d_recv,
):
    inbox = (inbox_first, inbox_second)
    dp = lax.axis_index("dp")
    mx = lax.axis_index("mx")
    my = lax.axis_index("my")
    core = lax.rem(dp, 2)
    high = lax.rem(dp // 2, 2)
    row = dp // 4
    core_peer = (dp + 1 - 2 * core, mx, my)
    high_peer = (row * 4 + (1 - high) * 2 + core, mx, my)

    def row_peer(step):
        return (lax.rem(row + step, 4) * 4 + lax.rem(dp, 4), mx, my)

    def x_peer(step):
        return (dp, mx, lax.rem(my + step, 4))

    turned = row * 4 + (1 - high) * 2 + core
    right = (jnp.where(mx == 3, turned, dp), lax.rem(mx + 1, 4), my)
    left = (jnp.where(mx == 0, turned, dp), lax.rem(mx + 3, 4), my)

    mine = pl.ds(pl.multiple_of(my * QUARTER, QUARTER), QUARTER)
    loads = (
        pltpu.make_async_copy(features.at[:, mine], given, load_sem.at[0]),
        pltpu.make_async_copy(w_out_given, w_out.at[:, :WIDE], load_sem.at[1]),
        pltpu.make_async_copy(w_qkv_given, w_qkv.at[:WIDE], load_sem.at[2]),
    )
    for load in loads:
        load.start()

    barrier = pltpu.get_barrier_semaphore()

    def greet(peer):
        pl.semaphore_signal(barrier, inc=1, device_id=peer, device_id_type=MESH)

    def dp_peer(step):
        return (lax.rem(dp + step, LOADERS), mx, my)

    for step in range(1, LOADERS):
        greet(dp_peer(step))
    for step in range(1, 4):
        greet(x_peer(step))

    greet(right)
    greet(left)
    greet((dp, lax.rem(mx + 2, 4), my))
    greet((turned, lax.rem(mx + 2, 4), my))
    def remote(src, dst, send, recv, peer):
        return pltpu.make_async_remote_copy(
            src_ref=src, dst_ref=dst, send_sem=send, recv_sem=recv,
            device_id=peer, device_id_type=MESH,
        )

    def tile_of(slot):
        ahead, which = SLOTS[slot]
        return 2 * lax.rem(mx + ahead + 4, 4) + which

    def crosses(slot):
        ahead = SLOTS[slot][0]
        return (mx + ahead < 0) | (mx + ahead > 3)

    def moves(slot, block):
        return (mx >= 0) if block else crosses(slot)

    def by_block(slot, block, values):
        chosen = values(0, 0)
        for source, (tile, turn) in ROUTES[slot, block].items():
            chosen = jnp.where(mx == source, values(tile, turn), chosen)
        return chosen

    def sent_tile(slot, block):
        return by_block(slot, block, lambda tile, turn: jnp.int32(tile))

    def opposite(block):
        return lax.rem(mx + 2 * block, 4)

    def sent_peer(slot, block):
        turn = by_block(slot, block, lambda tile, turn: jnp.int32(turn))
        return (jnp.where(turn == 1, turned, dp), opposite(block), my)

    def wave_of(kind, block):
        return pl.ds(block * WIDE + kind * WAVE, WAVE)

    def block_of(block):
        return pl.ds(block * WIDE, WIDE)

    def cross_copy(kind, slot, block):
        if kind < WAVES:
            src, dst = stage.at[kind, block, slot], feat.at[slot, mine, wave_of(kind, block)]
        else:
            src = cot_given.at[sent_tile(slot, block), mine]
            dst = cot.at[slot, mine, block_of(block)]
        return remote(
            src, dst, cross_send.at[kind, slot, block], cross_recv.at[kind, slot, block],
            sent_peer(slot, block),
        )

    def return_copy(slot, block):
        peer = (jnp.where(crosses(slot), turned, dp), opposite(block), my)
        return remote(
            back_out.at[slot, block], back_in.at[slot, block],
            cross_send.at[WAVES + 1, slot, block], cross_recv.at[WAVES + 1, slot, block], peer,
        )

    def spread_copy(kind, slot, block, step):
        if kind < WAVES:
            held = feat.at[slot, mine, wave_of(kind, block)]
        else:
            held = cot.at[slot, mine, block_of(block)]
        return remote(
            held, held, spread_send.at[kind, slot, block, step - 1],
            spread_recv.at[kind, slot, block, step - 1], x_peer(step),
        )

    def spread(kind, slot, block):
        for step in (2, 1, 3):
            spread_copy(kind, slot, block, step).start()

    def gather(kind, slot, block):
        for step in (1, 3, 2):
            spread_copy(kind, slot, block, step).wait_recv()

    def cot_load(slot):
        return pltpu.make_async_copy(
            cot_given.at[tile_of(slot)], cot.at[slot, :, block_of(0)], load_sem.at[3 + slot]
        )

    for slot in range(HELD):
        @pl.when(jnp.logical_not(crosses(slot)))
        def _():
            cot_load(slot).start()

    def weight_part(kind, index):
        lines = pl.ds(pl.multiple_of(index * PIECE, PIECE), PIECE)
        if kind == 0:
            return w_out.at[lines, block_of(1)]
        return w_qkv.at[pl.ds(pl.multiple_of(WIDE + index * PIECE, PIECE), PIECE)]

    own_part = 2 * row + core

    def w_far_copy(kind):
        lines = pl.ds(pl.multiple_of(own_part * PIECE, PIECE), PIECE)
        peer = (jnp.where(lax.rem(row, 2) == 0, dp, turned), opposite(1), my)
        return remote(
            (w_out_given, w_qkv_given)[kind].at[lines], weight_part(kind, own_part),
            w_far_send.at[kind], w_far_recv.at[kind], peer,
        )

    def w_row_copy(kind, step):
        held = weight_part(kind, own_part)
        return remote(
            held, held, w_row_send.at[kind, step - 1], w_row_recv.at[kind, step - 1],
            row_peer(step),
        )

    def w_core_copy(kind, step):
        held = weight_part(kind, 2 * lax.rem(row - step + 4, 4) + core)
        return remote(
            held, held, w_core_send.at[kind, step], w_core_recv.at[kind, step], core_peer
        )

    def w_spread(kind):
        w_far_copy(kind).wait_recv()
        for step in (2, 1, 3):
            w_row_copy(kind, step).start()
        w_core_copy(kind, 0).start()

    def w_share(kind):
        for step in (1, 3, 2):
            w_row_copy(kind, step).wait_recv()
            w_core_copy(kind, step).start()

    def w_wait(kind):
        for step in (0, 1, 3, 2):
            w_core_copy(kind, step).wait_recv()

    def position(loader, owner):
        place = jnp.int32(0)
        for tile in range(TILES):
            place = jnp.where(owners[loader, tile] == owner, tile, place)
        return place

    loads[0].wait()

    def fill(owner, carry):
        tile = position(dp, owner)
        for wave in range(WAVES):
            outbox[wave, owner] = given[tile, :, wave * WAVE : (wave + 1) * WAVE]
        return carry

    lax.fori_loop(0, LOADERS, fill, 0)

    def a_copy(wave, step):
        return remote(
            outbox.at[wave, lax.rem(dp + step, LOADERS)], inbox[wave].at[dp],
            a_send.at[wave, step - 1], a_recv.at[wave, step - 1], dp_peer(step),
        )

    def i_copy(step):
        return remote(
            given_ids, ids.at[dp], i_send.at[step - 1], i_recv.at[step - 1], dp_peer(step)
        )

    def send_wave(wave):
        for step in (2, 6, 10, 14, 1, 3, 5, 7, 9, 11, 13, 15, 4, 12, 8):
            a_copy(wave, step).start()

    for wave in range(WAVES):
        inbox[wave][dp] = outbox[wave, dp]
    ids[dp] = given_ids[...]
    pl.semaphore_wait(barrier, 22)
    for slot, block in MOVED:
        @pl.when(moves(slot, block))
        def _():
            cross_copy(WAVES, slot, block).start()

    w_far_copy(0).start()
    send_wave(0)
    w_far_copy(1).start()
    send_wave(1)
    for step in range(1, LOADERS):
        i_copy(step).start()

    loaders = [jnp.int32(0)] * TILES
    places = [jnp.int32(0)] * TILES
    count = jnp.int32(0)
    for loader in range(LOADERS):
        here = jnp.int32(0)
        for tile in range(TILES):
            here = jnp.where(owners[loader, tile] == dp, 1, here)
        place = position(loader, dp)
        for tile in range(TILES):
            fits = (here > 0) & (count == tile)
            loaders[tile] = jnp.where(fits, loader, loaders[tile])
            places[tile] = jnp.where(fits, place, places[tile])
        count = count + here

    def by_place(values, ahead, which):
        found_value = values[which]
        for place in range(4):
            found_value = jnp.where(
                lax.rem(mx + ahead + 4, 4) == place, values[2 * place + which], found_value
            )
        return found_value

    def picked(slot, block):
        return by_block(slot, block, lambda tile, turn: loaders[tile])

    def take_wave(wave):
        for step in range(1, LOADERS):
            a_copy(wave, step).wait_recv()
        if wave + 2 < WAVES:
            send_wave(wave + 2)
        for slot, block in MOVED:
            @pl.when(moves(slot, block))
            def _():
                stage[wave, block, slot] = inbox[wave][picked(slot, block)]
                cross_copy(wave, slot, block).start()

        for slot in (2, 3, 0, 1):
            @pl.when(jnp.logical_not(crosses(slot)))
            def _():
                feat[slot, mine, wave * WAVE : (wave + 1) * WAVE] = inbox[wave][
                    by_place(loaders, *SLOTS[slot])
                ]
                spread(wave, slot, 0)

    def spread_moved(kind):
        for slot, block in MOVED:
            @pl.when(moves(slot, block))
            def _():
                cross_copy(kind, slot, block).wait_recv()
                spread(kind, slot, block)

    def make_masks():
        for step in range(1, LOADERS):
            i_copy(step).wait_recv()
        for tile in range(2):
            loader = by_place(loaders, 0, tile)
            place = by_place(places, 0, tile)
            line = ids[loader, pl.ds(place, 1), :].astype(F32)
            across = jnp.broadcast_to(line, (PATCH, PATCH))
            mask[tile] = (across == across.T).astype(F32)

    def project_back(unit):
        half = unit // HALF
        tiles = pl.ds(2 * lax.rem(unit, HALF), 2)
        lines = pl.ds(pl.multiple_of(half * QKV, HEAD), QKV)
        product = dot(cot[tiles].reshape(2 * PATCH, BOTH), w_out[lines, :], NT).astype(BF)
        part[half, tiles] = product.reshape(2, PATCH, QKV)

    def project(unit):
        group = unit // HALF
        tiles = pl.ds(2 * lax.rem(unit, HALF), 2)
        columns = pl.ds(pl.multiple_of((group - 2) * QKV, HEAD), QKV)
        product = dot(feat[tiles].reshape(2 * PATCH, BOTH), w_qkv[:, columns], NN).astype(BF)
        part[group, tiles] = product.reshape(2, PATCH, QKV)

    def run(function, start, stop):
        def step(unit, carry):
            function(unit)
            return carry

        lax.fori_loop(start, stop, step, 0)

    def b_copy(group, which):
        return remote(
            part.at[group, 2 + which], chain.at[group, which],
            b_send.at[group, which], b_recv.at[group, which], (left, right)[which],
        )

    def c_copy(head, which):
        return remote(
            found.at[head, which], found.at[head, 2 + which],
            c_send.at[head, which], c_recv.at[head, which], (right, left)[which],
        )

    def b_first(group):
        for which in range(2):
            b_copy(group, which).start()

    def b_total(group, which):
        b_copy(group, which).wait_recv()
        return part[group, which].astype(F32) + chain[group, which].astype(F32)

    def c_first(head):
        for which in range(2):
            c_copy(head, which).start()

    def attend_head(head):
        columns = pl.ds(pl.multiple_of(lax.rem(head, 3) * HEAD, HEAD), HEAD)
        totals = [b_total(head + 2, tile) for tile in range(2)]
        for tile in range(2):
            found[head, tile] = attend(
                totals[tile], part[head // 3, tile, :, columns], mask[tile]
            )
        c_first(head)

    spread_moved(WAVES)
    w_spread(0)
    for wave in range(WAVES):
        take_wave(wave)
        if wave == 0:
            w_spread(1)
        else:
            spread_moved(wave - 1)
    w_share(0)
    spread_moved(WAVES - 1)
    w_share(1)
    make_masks()
    for slot in range(HELD):
        @pl.when(jnp.logical_not(crosses(slot)))
        def _():
            cot_load(slot).wait()

    for slot, block in MOVED:
        @pl.when(moves(slot, block))
        def _():
            gather(WAVES, slot, block)

    loads[1].wait()
    w_wait(0)
    run(project_back, 0, BACKS)
    for group in range(2):
        b_first(group)
    for wave in range(WAVES):
        for slot in range(HELD):
            for block in range(2):
                gather(wave, slot, block)
    loads[2].wait()
    w_wait(1)
    run(project, BACKS, BACKS + HALF)
    b_first(2)
    for group in range(2):
        for tile in range(2):
            part[group, tile] = b_total(group, tile).astype(BF)

    feat_acc[...] = jnp.zeros_like(feat_acc)

    def core_copy(chunk):
        return remote(
            grads.at[chunk, :, :, 1 - core], core_in.at[chunk],
            core_send.at[chunk], core_recv.at[chunk], core_peer,
        )

    def y_copy(chunk, step):
        return remote(
            core_sum.at[chunk, :, pl.ds(2 * lax.rem(row + step, 4), 2)], y_in.at[chunk, step - 1],
            y_send.at[chunk, step - 1], y_recv.at[chunk, step - 1], row_peer(step),
        )

    def high_peers(which):
        return (high_peer, (dp, opposite(1), my), (turned, opposite(1), my))[which]

    def high_part(held, which):
        return (held.at[0, 1 - high], held.at[1, high], held.at[1, 1 - high])[which]

    def z_copy(chunk, which):
        return remote(
            high_part(y_sum.at[chunk], which), z_in.at[chunk, which],
            z_send.at[chunk, which], z_recv.at[chunk, which], high_peers(which),
        )

    def stage_core(chunk):
        core_copy(chunk).wait_recv()
        core_sum[chunk] = (
            grads[chunk, :, :, core].astype(F32) + core_in[chunk].astype(F32)
        ).astype(BF)
        for step in (2, 1, 3):
            y_copy(chunk, step).start()

    def stage_row(chunk):
        total = core_sum[chunk, :, pl.ds(2 * row, 2)].astype(F32)
        for step in (1, 3, 2):
            y_copy(chunk, step).wait_recv()
            total = total + y_in[chunk, step - 1].astype(F32)
        y_sum[chunk] = total.astype(BF)
        for which in range(3):
            z_copy(chunk, which).start()

    def stage_high(chunk):
        total = y_sum[chunk, 0, high].astype(F32)
        for which in (1, 2, 0):
            z_copy(chunk, which).wait_recv()
            total = total + z_in[chunk, which].astype(F32)
        return total * (1.0 / 16.0)

    def store_qkv(chunk):
        columns = pl.ds(pl.multiple_of(chunk * QKV, HEAD), QKV)
        out_qkv[0, :, columns] = stage_high(chunk)

    def back_pair(head, pair):
        tiles = pl.ds(2 * pair, 2)
        columns = pl.ds(pl.multiple_of(head * QKV, HEAD), QKV)
        back = dot(found[head, tiles, :, HEAD:].reshape(2 * PATCH, QKV), w_qkv[:, columns], NT)
        feat_acc[tiles] += back.reshape(2, PATCH, BOTH)

    def d_copy(pair, step):
        lines = pl.ds(pl.multiple_of(lax.rem(my + step, 4) * QUARTER, QUARTER), QUARTER)
        tiles = pl.ds(2 * pair, 2)
        return remote(
            feat_bf.at[tiles, lines], feat_in.at[step - 1, tiles],
            d_send.at[pair, step - 1], d_recv.at[pair, step - 1], x_peer(step),
        )

    def d_start(pair):
        tiles = pl.ds(2 * pair, 2)
        feat_bf[tiles] = feat_acc[tiles].astype(BF)
        for step in (2, 1, 3):
            d_copy(pair, step).start()

    def d_finish(pair):
        for step in (1, 3, 2):
            d_copy(pair, step).wait_recv()
        for slot in (2 * pair, 2 * pair + 1):
            total = feat_acc[slot, mine, :]
            for step in (1, 3, 2):
                total = total + feat_in[step - 1, slot].astype(F32)
            total = total.astype(BF)
            for block in (1, 0):
                @pl.when(moves(slot, block))
                def _():
                    back_out[slot, block] = total[:, block * WIDE : (block + 1) * WIDE]
                    return_copy(slot, block).start()

            @pl.when(jnp.logical_not(crosses(slot)))
            def _():
                out_feat[tile_of(slot)] = total[:, :WIDE]

    def half_core_copy(half):
        return remote(
            half_grad.at[half, :, :, 1 - core], half_in.at[half],
            half_core_send.at[half], half_core_recv.at[half], core_peer,
        )

    def half_row_copy(step):
        to = lax.rem(row + step, 4)
        return remote(
            half_sum.at[to // 2, :, pl.ds(2 * lax.rem(to, 2), 2)], half_y.at[step - 1],
            half_row_send.at[step - 1], half_row_recv.at[step - 1], row_peer(step),
        )

    def half_high_copy(which):
        return remote(
            high_part(half_ysum, which), half_z.at[which],
            half_high_send.at[which], half_high_recv.at[which], high_peers(which),
        )

    def half_begin(half):
        lines = slice(half * HALF_ROWS, (half + 1) * HALF_ROWS)
        for block in range(2):
            half_grad[half, block] = grad_wide[
                lines, block * WIDE : (block + 1) * WIDE
            ].reshape(4, 2, 48, WIDE)
        half_core_copy(half).start()

    def half_stage_core(half):
        half_core_copy(half).wait_recv()
        half_sum[half] = (
            half_grad[half, :, :, core].astype(F32) + half_in[half].astype(F32)
        ).astype(BF)
        for step in (2, 1, 3):
            @pl.when(lax.rem(row + step, 4) // 2 == half)
            def _():
                half_row_copy(step).start()

    def half_stage_row(half):
        @pl.when(row // 2 == half)
        def _():
            total = half_sum[half, :, pl.ds(2 * lax.rem(row, 2), 2)].astype(F32)
            for step in (1, 3, 2):
                half_row_copy(step).wait_recv()
                total = total + half_y[step - 1].astype(F32)
            half_ysum[...] = total.astype(BF)
            for which in range(3):
                half_high_copy(which).start()

    def half_stage_high(half):
        @pl.when(row // 2 == half)
        def _():
            total = half_ysum[0, high].astype(F32)
            for which in (1, 2, 0):
                half_high_copy(which).wait_recv()
                total = total + half_z[which].astype(F32)
            out_out[0] = total * (1.0 / 16.0)

    def weight_piece(head, at):
        grad = found[head, :, :, HEAD:].reshape(HELD * PATCH, QKV)
        lines = pl.ds(pl.multiple_of(at * HALF_ROWS, HALF_ROWS), HALF_ROWS)
        piece = dot(feat_t[lines, :], grad, NN).astype(BF)
        grads[head, at // 2, pl.ds(4 * lax.rem(at, 2), 4)] = piece.reshape(4, 2, 48, QKV)

    def weights(head):
        lines = pl.ds(pl.multiple_of(head * HEAD, HEAD), HEAD)
        grad_wide[lines, :] = dot(
            found[head, :, :, :HEAD].reshape(HELD * PATCH, HEAD),
            cot[...].reshape(HELD * PATCH, BOTH),
            TN,
        ).astype(BF)
        for half in range(2):
            @pl.when(head == 3 * half + 2)
            def _():
                half_begin(half)

        run(lambda at: weight_piece(head, at), 0, 4)
        core_copy(head).start()

    def near_rows(head):
        back_pair(head, 0)

        @pl.when(head == HEADS_HERE - 1)
        def _():
            d_start(0)

    def far_rows(head):
        for which in range(2):
            c_copy(head, which).wait_recv()
        back_pair(head, 1)

        @pl.when(head == HEADS_HERE - 1)
        def _():
            d_start(1)

    def when(least, head, function):
        @pl.when((head >= least) & (head < HEADS_HERE))
        def _():
            function(head)

    def head_step(now):
        when(1, now, lambda head: b_first(head + 2))
        when(1, now + 1, lambda head: run(project, BACKS + HALF * head, BACKS + HALF * head + HALF))
        when(0, now - 1, attend_head)

        @pl.when(now < 2)
        def _():
            for slot in range(2):
                columns = pl.ds(pl.multiple_of((2 * now + slot) * PATCH, PATCH), PATCH)
                feat_t[:, columns] = feat[2 * now + slot].T

        @pl.when(now >= 3)
        def _():
            stage_core(now - 3)

        @pl.when(now >= 5)
        def _():
            stage_row(now - 5)

        @pl.when(now >= 6)
        def _():
            store_qkv(now - 6)

        for later, stage_half in ((5, half_stage_core), (7, half_stage_row)):
            @pl.when(now == later)
            def _():
                stage_half(0)

        when(0, now - 1, near_rows)
        when(0, now - 2, far_rows)
        when(0, now - 2, weights)

    run(head_step, 0, HEADS_HERE + 2)

    half_stage_core(1)
    stage_core(5)
    d_finish(0)
    stage_row(3)
    store_qkv(2)
    d_finish(1)
    stage_row(4)
    half_stage_row(1)
    store_qkv(3)
    half_stage_high(0)
    stage_row(5)
    store_qkv(4)
    half_stage_high(1)
    store_qkv(5)
    for slot, block in MOVED:
        @pl.when(moves(slot, block))
        def _():
            return_copy(slot, block).wait_recv()
            out_feat[sent_tile(slot, block)] = back_in[slot, block]

    for step in range(1, LOADERS):
        for wave in range(WAVES):
            a_copy(wave, step).wait_send()
        i_copy(step).wait_send()
    for step in range(1, 4):
        for pair in range(2):
            d_copy(pair, step).wait_send()
        half_row_copy(step).wait_send()
    for half in range(2):
        half_core_copy(half).wait_send()
    for which in range(3):
        half_high_copy(which).wait_send()
    for slot, block in MOVED:
        @pl.when(moves(slot, block))
        def _():
            for kind in range(WAVES + 1):
                cross_copy(kind, slot, block).wait_send()
            return_copy(slot, block).wait_send()
            for step in range(1, 4):
                spread_copy(WAVES, slot, block, step).wait_send()

        for step in range(1, 4):
            for wave in range(WAVES):
                spread_copy(wave, slot, block, step).wait_send()
    for kind in range(2):
        w_far_copy(kind).wait_send()
        for step in range(4):
            w_core_copy(kind, step).wait_send()
        for step in range(1, 4):
            w_row_copy(kind, step).wait_send()

    def drain(chunk, carry):
        core_copy(chunk).wait_send()
        for which in range(3):
            z_copy(chunk, which).wait_send()
        for step in range(1, 4):
            y_copy(chunk, step).wait_send()
        return carry

    lax.fori_loop(0, CHUNKS, drain, 0)

    def drain_group(group):
        for which in range(2):
            b_copy(group, which).wait_send()

    def drain_head(head):
        for which in range(2):
            c_copy(head, which).wait_send()

    run(drain_group, 0, GROUPS)
    run(drain_head, 0, HEADS_HERE)


def shards(features, segment_ids, owners, w_qkv, w_out, cotangent):
    vmem = pl.BlockSpec(memory_space=pltpu.VMEM)
    hbm = pl.BlockSpec(memory_space=pl.ANY)
    smem = pl.BlockSpec(memory_space=pltpu.SMEM)
    dma = pltpu.SemaphoreType.DMA
    units = (HEADS_HERE, TILES, PATCH, UNIT)
    sums = (GROUPS, TILES, PATCH, QKV)
    return pl.pallas_call(
        branch,
        out_shape=(
            jax.ShapeDtypeStruct((TILES, 32, WIDE), BF),
            jax.ShapeDtypeStruct((1, 48, HEADS_HERE * QKV), F32),
            jax.ShapeDtypeStruct((1, 48, WIDE), F32),
        ),
        in_specs=[smem, hbm, vmem, hbm, hbm, hbm],
        out_specs=(vmem,) * 3,
        scratch_shapes=[
            pltpu.VMEM((TILES, QUARTER, WIDE), BF),
            pltpu.VMEM((BOTH, HEADS_HERE * QKV), BF),
            pltpu.VMEM((HEADS_HERE * HEAD, BOTH), BF),
            dma((3 + HELD,)),
            pltpu.VMEM((HELD, PATCH, BOTH), BF),
            pltpu.VMEM((HELD, PATCH, BOTH), BF),
            pltpu.VMEM((BOTH, HELD * PATCH), BF),
            pltpu.VMEM((GROUPS, HELD, PATCH, QKV), BF),
            pltpu.VMEM((GROUPS, 2, PATCH, QKV), BF),
            pltpu.VMEM((HEADS_HERE, HELD, PATCH, UNIT), BF),
            pltpu.VMEM((CHUNKS, 2, 8, 2, 48, QKV), BF),
            pltpu.VMEM((CHUNKS, 2, 8, 48, QKV), BF),
            pltpu.VMEM((CHUNKS, 2, 8, 48, QKV), BF),
            pltpu.VMEM((CHUNKS, 3, 2, 2, 48, QKV), BF),
            pltpu.VMEM((CHUNKS, 2, 2, 48, QKV), BF),
            pltpu.VMEM((CHUNKS, 3, 48, QKV), BF),
            pltpu.VMEM((2, 2, 4, 2, 48, WIDE), BF),
            pltpu.VMEM((2, 2, 4, 48, WIDE), BF),
            pltpu.VMEM((2, 2, 4, 48, WIDE), BF),
            pltpu.VMEM((3, 2, 2, 48, WIDE), BF),
            pltpu.VMEM((2, 2, 48, WIDE), BF),
            pltpu.VMEM((3, 48, WIDE), BF),
            pltpu.VMEM((WIDE, BOTH), BF),
            pltpu.VMEM((HELD, PATCH, BOTH), F32),
            pltpu.VMEM((HELD, PATCH, BOTH), BF),
            pltpu.VMEM((3, HELD, QUARTER, BOTH), BF),
            pltpu.VMEM((WAVES, LOADERS, QUARTER, WAVE), BF),
            pltpu.VMEM((LOADERS, QUARTER, WAVE), BF),
            pltpu.VMEM((LOADERS, QUARTER, WAVE), BF),
            pltpu.VMEM((LOADERS, TILES, PATCH), jnp.int32),
            pltpu.VMEM((2, PATCH, PATCH), F32),
            dma((2,)), dma((2,)), dma((2, 3)), dma((2, 3)), dma((2, 4)), dma((2, 4)),
            pltpu.VMEM((WAVES, 2, HELD, QUARTER, WAVE), BF),
            pltpu.VMEM((HELD, 2, QUARTER, WIDE), BF),
            pltpu.VMEM((HELD, 2, QUARTER, WIDE), BF),
            dma((WAVES + 2, HELD, 2)), dma((WAVES + 2, HELD, 2)),
            dma((WAVES + 1, HELD, 2, 3)), dma((WAVES + 1, HELD, 2, 3)),
            dma((WAVES, LOADERS - 1)), dma((WAVES, LOADERS - 1)),
            dma((LOADERS - 1,)), dma((LOADERS - 1,)),
            dma((GROUPS, 2)), dma((GROUPS, 2)),
            dma((HEADS_HERE, 2)), dma((HEADS_HERE, 2)),
            dma((2,)), dma((2,)), dma((3,)), dma((3,)), dma((3,)), dma((3,)),
            dma((CHUNKS,)), dma((CHUNKS,)),
            dma((CHUNKS, 3)), dma((CHUNKS, 3)),
            dma((CHUNKS, 3)), dma((CHUNKS, 3)),
            dma((2, 3)), dma((2, 3)),
        ],
        compiler_params=pltpu.CompilerParams(
            collective_id=0, has_side_effects=True, vmem_limit_bytes=60 * 1024 * 1024
        ),
        cost_estimate=pl.CostEstimate(
            flops=14_000_000_000, bytes_accessed=12_000_000, transcendentals=400_000
        ),
    )(owners, features, segment_ids, cotangent, w_qkv, w_out)


def solution(mesh):
    return jax.shard_map(
        shards,
        mesh=mesh,
        in_specs=(
            P("dp", None, "mx"),
            P("dp", None),
            P(),
            P("mx", "my"),
            P("my", "mx"),
            P("dp", None, "mx"),
        ),
        out_specs=(P("dp", "my", "mx"), P("mx", "dp", "my"), P("my", "dp", "mx")),
        check_vma=False,
    )
```

```python
import jax
import jax.numpy as jnp
from jax import lax
from jax.experimental import pallas as pl
from jax.experimental.pallas import tpu as pltpu
from jax.sharding import PartitionSpec as P

HEAD = 128
HEADS_HERE = 6
TILES = 8
HALF = 2
HELD = 4
BOTH = 2 * 768
PIECE = 96
GROUPS = HEADS_HERE + 2
BACKS = 2 * HALF
LOADERS = 16
QUARTER = 32
PATCH = 128
WIDE = 768
QKV = 3 * HEAD
UNIT = QKV + HEAD
CHUNKS = HEADS_HERE
HALF_ROWS = 384
SLOTS = ((0, 0), (0, 1), (-1, 0), (1, 1))


def routes():
    table = {}
    for block in range(4):
        for place in range(4):
            for which in range(2):
                off = 0 if (place - block) % 2 == 0 else 1 - 2 * which
                to = place + off
                slot = which if off == 0 else 2 + which
                table.setdefault((slot, int(to % 4 != block)), {})[block] = (
                    2 * place + which, int(not 0 <= to <= 3)
                )
    return table


ROUTES = routes()
MOVED = tuple((slot, block) for block in (1, 0) for slot in range(4))
WAVES = 2
WAVE = WIDE // WAVES
BF = jnp.bfloat16
F32 = jnp.float32
MESH = pl.DeviceIdType.MESH
SCALE = HEAD ** (-0.5)


def dot(a, b, contract):
    return lax.dot_general(a, b, ((contract[0], contract[1]), ((), ())), preferred_element_type=F32)


NN = ((1,), (0,))
NT = ((1,), (1,))
TN = ((0,), (0,))


def normalize(values):
    centered = values - jnp.mean(values, axis=-1, keepdims=True)
    inverse = lax.rsqrt(jnp.mean(centered * centered, axis=-1, keepdims=True) + 1e-06)
    return centered * inverse, inverse


def norm_back(grad_hat, normed, inverse):
    return inverse * (
        grad_hat
        - jnp.mean(grad_hat, axis=-1, keepdims=True)
        - normed * jnp.mean(grad_hat * normed, axis=-1, keepdims=True)
    )


def attend(total, grad_bf, mask):
    query_hat, query_inv = normalize(total[:, :HEAD])
    key_hat, key_inv = normalize(total[:, HEAD : 2 * HEAD])
    query_bf = query_hat.astype(BF)
    key_bf = key_hat.astype(BF)
    value_bf = total[:, 2 * HEAD :].astype(BF)
    expo = jnp.exp(dot(query_bf, key_bf, NT) * SCALE) * mask
    weights = expo / jnp.sum(expo, axis=-1, keepdims=True)
    weights_bf = weights.astype(BF)
    attended = dot(weights_bf, value_bf, NN)
    grad_value = dot(weights_bf, grad_bf, TN)
    grad_weights = dot(grad_bf, value_bf, NT)
    grad_scores = (
        weights
        * (grad_weights - jnp.sum(weights * grad_weights, axis=-1, keepdims=True))
        * SCALE
    ).astype(BF)
    grad_query = norm_back(dot(grad_scores, key_bf, NN), query_hat, query_inv)
    grad_key = norm_back(dot(grad_scores, query_bf, TN), key_hat, key_inv)
    return jnp.concatenate([attended, grad_query, grad_key, grad_value], axis=1).astype(BF)


def branch(
    owners, features, given_ids, cot_given, w_qkv_given, w_out_given,
    out_feat, out_qkv, out_out,
    given, w_qkv, w_out, load_sem, feat, cot, feat_t, part, chain, found, grads, core_in, core_sum, y_in, y_sum, z_in,
    half_grad, half_in, half_sum, half_y, half_ysum, half_z, grad_wide, feat_acc, feat_bf, feat_in, outbox, inbox_first, inbox_second, ids, mask,
    w_far_send, w_far_recv, w_row_send, w_row_recv, w_core_send, w_core_recv,
    stage, back_out, back_in, cross_send, cross_recv, spread_send, spread_recv,
    a_send, a_recv, i_send, i_recv, b_send, b_recv, c_send, c_recv,
    half_core_send, half_core_recv, half_row_send, half_row_recv, half_high_send, half_high_recv,
    core_send, core_recv, y_send, y_recv, z_send, z_recv, d_send, d_recv,
):
    inbox = (inbox_first, inbox_second)
    dp = lax.axis_index("dp")
    mx = lax.axis_index("mx")
    my = lax.axis_index("my")
    core = lax.rem(dp, 2)
    high = lax.rem(dp // 2, 2)
    row = dp // 4
    core_peer = (dp + 1 - 2 * core, mx, my)
    high_peer = (row * 4 + (1 - high) * 2 + core, mx, my)

    def row_peer(step):
        return (lax.rem(row + step, 4) * 4 + lax.rem(dp, 4), mx, my)

    def x_peer(step):
        return (dp, mx, lax.rem(my + step, 4))

    turned = row * 4 + (1 - high) * 2 + core
    right = (jnp.where(mx == 3, turned, dp), lax.rem(mx + 1, 4), my)
    left = (jnp.where(mx == 0, turned, dp), lax.rem(mx + 3, 4), my)

    mine = pl.ds(pl.multiple_of(my * QUARTER, QUARTER), QUARTER)
    loads = (
        pltpu.make_async_copy(features.at[:, mine], given, load_sem.at[0]),
        pltpu.make_async_copy(w_out_given, w_out.at[:, :WIDE], load_sem.at[1]),
        pltpu.make_async_copy(w_qkv_given, w_qkv.at[:WIDE], load_sem.at[2]),
    )
    for load in loads:
        load.start()

    barrier = pltpu.get_barrier_semaphore()

    def greet(peer):
        pl.semaphore_signal(barrier, inc=1, device_id=peer, device_id_type=MESH)

    def dp_peer(step):
        return (lax.rem(dp + step, LOADERS), mx, my)

    for step in range(1, LOADERS):
        greet(dp_peer(step))
    for step in range(1, 4):
        greet(x_peer(step))

    greet(right)
    greet(left)
    greet((dp, lax.rem(mx + 2, 4), my))
    greet((turned, lax.rem(mx + 2, 4), my))
    def remote(src, dst, send, recv, peer):
        return pltpu.make_async_remote_copy(
            src_ref=src, dst_ref=dst, send_sem=send, recv_sem=recv,
            device_id=peer, device_id_type=MESH,
        )

    def tile_of(slot):
        ahead, which = SLOTS[slot]
        return 2 * lax.rem(mx + ahead + 4, 4) + which

    def crosses(slot):
        ahead = SLOTS[slot][0]
        return (mx + ahead < 0) | (mx + ahead > 3)

    def moves(slot, block):
        return (mx >= 0) if block else crosses(slot)

    def by_block(slot, block, values):
        chosen = values(0, 0)
        for source, (tile, turn) in ROUTES[slot, block].items():
            chosen = jnp.where(mx == source, values(tile, turn), chosen)
        return chosen

    def sent_tile(slot, block):
        return by_block(slot, block, lambda tile, turn: jnp.int32(tile))

    def opposite(block):
        return lax.rem(mx + 2 * block, 4)

    def sent_peer(slot, block):
        turn = by_block(slot, block, lambda tile, turn: jnp.int32(turn))
        return (jnp.where(turn == 1, turned, dp), opposite(block), my)

    def wave_of(kind, block):
        return pl.ds(block * WIDE + kind * WAVE, WAVE)

    def block_of(block):
        return pl.ds(block * WIDE, WIDE)

    def cross_copy(kind, slot, block):
        if kind < WAVES:
            src, dst = stage.at[kind, block, slot], feat.at[slot, mine, wave_of(kind, block)]
        else:
            src = cot_given.at[sent_tile(slot, block), mine]
            dst = cot.at[slot, mine, block_of(block)]
        return remote(
            src, dst, cross_send.at[kind, slot, block], cross_recv.at[kind, slot, block],
            sent_peer(slot, block),
        )

    def return_copy(slot, block):
        peer = (jnp.where(crosses(slot), turned, dp), opposite(block), my)
        return remote(
            back_out.at[slot, block], back_in.at[slot, block],
            cross_send.at[WAVES + 1, slot, block], cross_recv.at[WAVES + 1, slot, block], peer,
        )

    def spread_copy(kind, slot, block, step):
        if kind < WAVES:
            held = feat.at[slot, mine, wave_of(kind, block)]
        else:
            held = cot.at[slot, mine, block_of(block)]
        return remote(
            held, held, spread_send.at[kind, slot, block, step - 1],
            spread_recv.at[kind, slot, block, step - 1], x_peer(step),
        )

    def spread(kind, slot, block):
        for step in (2, 1, 3):
            spread_copy(kind, slot, block, step).start()

    def gather(kind, slot, block):
        for step in (1, 3, 2):
            spread_copy(kind, slot, block, step).wait_recv()

    def cot_load(slot):
        return pltpu.make_async_copy(
            cot_given.at[tile_of(slot)], cot.at[slot, :, block_of(0)], load_sem.at[3 + slot]
        )

    for slot in range(HELD):
        @pl.when(jnp.logical_not(crosses(slot)))
        def _():
            cot_load(slot).start()

    def weight_part(kind, index):
        lines = pl.ds(pl.multiple_of(index * PIECE, PIECE), PIECE)
        if kind == 0:
            return w_out.at[lines, block_of(1)]
        return w_qkv.at[pl.ds(pl.multiple_of(WIDE + index * PIECE, PIECE), PIECE)]

    own_part = 2 * row + core

    def w_far_copy(kind):
        lines = pl.ds(pl.multiple_of(own_part * PIECE, PIECE), PIECE)
        peer = (jnp.where(lax.rem(row, 2) == 0, dp, turned), opposite(1), my)
        return remote(
            (w_out_given, w_qkv_given)[kind].at[lines], weight_part(kind, own_part),
            w_far_send.at[kind], w_far_recv.at[kind], peer,
        )

    def w_row_copy(kind, step):
        held = weight_part(kind, own_part)
        return remote(
            held, held, w_row_send.at[kind, step - 1], w_row_recv.at[kind, step - 1],
            row_peer(step),
        )

    def w_core_copy(kind, step):
        held = weight_part(kind, 2 * lax.rem(row - step + 4, 4) + core)
        return remote(
            held, held, w_core_send.at[kind, step], w_core_recv.at[kind, step], core_peer
        )

    def w_spread(kind):
        w_far_copy(kind).wait_recv()
        for step in (2, 1, 3):
            w_row_copy(kind, step).start()
        w_core_copy(kind, 0).start()

    def w_share(kind):
        for step in (1, 3, 2):
            w_row_copy(kind, step).wait_recv()
            w_core_copy(kind, step).start()

    def w_wait(kind):
        for step in (0, 1, 3, 2):
            w_core_copy(kind, step).wait_recv()

    def position(loader, owner):
        place = jnp.int32(0)
        for tile in range(TILES):
            place = jnp.where(owners[loader, tile] == owner, tile, place)
        return place

    loads[0].wait()

    def fill(owner, carry):
        tile = position(dp, owner)
        for wave in range(WAVES):
            outbox[wave, owner] = given[tile, :, wave * WAVE : (wave + 1) * WAVE]
        return carry

    lax.fori_loop(0, LOADERS, fill, 0)

    def a_copy(wave, step):
        return remote(
            outbox.at[wave, lax.rem(dp + step, LOADERS)], inbox[wave].at[dp],
            a_send.at[wave, step - 1], a_recv.at[wave, step - 1], dp_peer(step),
        )

    def i_copy(step):
        return remote(
            given_ids, ids.at[dp], i_send.at[step - 1], i_recv.at[step - 1], dp_peer(step)
        )

    def send_wave(wave):
        for step in (2, 6, 10, 14, 1, 3, 5, 7, 9, 11, 13, 15, 4, 12, 8):
            a_copy(wave, step).start()

    for wave in range(WAVES):
        inbox[wave][dp] = outbox[wave, dp]
    ids[dp] = given_ids[...]
    pl.semaphore_wait(barrier, 22)
    for slot, block in MOVED:
        @pl.when(moves(slot, block))
        def _():
            cross_copy(WAVES, slot, block).start()

    w_far_copy(0).start()
    send_wave(0)
    w_far_copy(1).start()
    send_wave(1)
    for step in range(1, LOADERS):
        i_copy(step).start()

    loaders = [jnp.int32(0)] * TILES
    places = [jnp.int32(0)] * TILES
    count = jnp.int32(0)
    for loader in range(LOADERS):
        here = jnp.int32(0)
        for tile in range(TILES):
            here = jnp.where(owners[loader, tile] == dp, 1, here)
        place = position(loader, dp)
        for tile in range(TILES):
            fits = (here > 0) & (count == tile)
            loaders[tile] = jnp.where(fits, loader, loaders[tile])
            places[tile] = jnp.where(fits, place, places[tile])
        count = count + here

    def by_place(values, ahead, which):
        found_value = values[which]
        for place in range(4):
            found_value = jnp.where(
                lax.rem(mx + ahead + 4, 4) == place, values[2 * place + which], found_value
            )
        return found_value

    def picked(slot, block):
        return by_block(slot, block, lambda tile, turn: loaders[tile])

    def take_wave(wave):
        for step in range(1, LOADERS):
            a_copy(wave, step).wait_recv()
        if wave + 2 < WAVES:
            send_wave(wave + 2)
        for slot, block in MOVED:
            @pl.when(moves(slot, block))
            def _():
                stage[wave, block, slot] = inbox[wave][picked(slot, block)]
                cross_copy(wave, slot, block).start()

        for slot in (2, 3, 0, 1):
            @pl.when(jnp.logical_not(crosses(slot)))
            def _():
                feat[slot, mine, wave * WAVE : (wave + 1) * WAVE] = inbox[wave][
                    by_place(loaders, *SLOTS[slot])
                ]
                spread(wave, slot, 0)

    def spread_moved(kind):
        for slot, block in MOVED:
            @pl.when(moves(slot, block))
            def _():
                cross_copy(kind, slot, block).wait_recv()
                spread(kind, slot, block)

    def make_masks():
        for step in range(1, LOADERS):
            i_copy(step).wait_recv()
        for tile in range(2):
            loader = by_place(loaders, 0, tile)
            place = by_place(places, 0, tile)
            line = ids[loader, pl.ds(place, 1), :].astype(F32)
            across = jnp.broadcast_to(line, (PATCH, PATCH))
            mask[tile] = (across == across.T).astype(F32)

    def project_back(unit):
        half = unit // HALF
        tiles = pl.ds(2 * lax.rem(unit, HALF), 2)
        lines = pl.ds(pl.multiple_of(half * QKV, HEAD), QKV)
        product = dot(cot[tiles].reshape(2 * PATCH, BOTH), w_out[lines, :], NT).astype(BF)
        part[half, tiles] = product.reshape(2, PATCH, QKV)

    def project(unit):
        group = unit // HALF
        tiles = pl.ds(2 * lax.rem(unit, HALF), 2)
        columns = pl.ds(pl.multiple_of((group - 2) * QKV, HEAD), QKV)
        product = dot(feat[tiles].reshape(2 * PATCH, BOTH), w_qkv[:, columns], NN).astype(BF)
        part[group, tiles] = product.reshape(2, PATCH, QKV)

    def run(function, start, stop):
        def step(unit, carry):
            function(unit)
            return carry

        lax.fori_loop(start, stop, step, 0)

    def b_copy(group, which):
        return remote(
            part.at[group, 2 + which], chain.at[group, which],
            b_send.at[group, which], b_recv.at[group, which], (left, right)[which],
        )

    def c_copy(head, which):
        return remote(
            found.at[head, which], found.at[head, 2 + which],
            c_send.at[head, which], c_recv.at[head, which], (right, left)[which],
        )

    def b_first(group):
        for which in range(2):
            b_copy(group, which).start()

    def b_total(group, which):
        b_copy(group, which).wait_recv()
        return part[group, which].astype(F32) + chain[group, which].astype(F32)

    def c_first(head):
        for which in range(2):
            c_copy(head, which).start()

    def attend_head(head):
        columns = pl.ds(pl.multiple_of(lax.rem(head, 3) * HEAD, HEAD), HEAD)
        totals = [b_total(head + 2, tile) for tile in range(2)]
        for tile in range(2):
            found[head, tile] = attend(
                totals[tile], part[head // 3, tile, :, columns], mask[tile]
            )
        c_first(head)

    spread_moved(WAVES)
    w_spread(0)
    for wave in range(WAVES):
        take_wave(wave)
        if wave == 0:
            w_spread(1)
        else:
            spread_moved(wave - 1)
    w_share(0)
    spread_moved(WAVES - 1)
    w_share(1)
    make_masks()
    for slot in range(HELD):
        @pl.when(jnp.logical_not(crosses(slot)))
        def _():
            cot_load(slot).wait()

    for slot, block in MOVED:
        @pl.when(moves(slot, block))
        def _():
            gather(WAVES, slot, block)

    loads[1].wait()
    w_wait(0)
    run(project_back, 0, BACKS)
    for group in range(2):
        b_first(group)
    for wave in range(WAVES):
        for slot in range(HELD):
            for block in range(2):
                gather(wave, slot, block)
    loads[2].wait()
    w_wait(1)
    run(project, BACKS, BACKS + HALF)
    b_first(2)
    for group in range(2):
        for tile in range(2):
            part[group, tile] = b_total(group, tile).astype(BF)

    feat_acc[...] = jnp.zeros_like(feat_acc)

    def core_copy(chunk):
        return remote(
            grads.at[chunk, :, :, 1 - core], core_in.at[chunk],
            core_send.at[chunk], core_recv.at[chunk], core_peer,
        )

    def y_copy(chunk, step):
        return remote(
            core_sum.at[chunk, :, pl.ds(2 * lax.rem(row + step, 4), 2)], y_in.at[chunk, step - 1],
            y_send.at[chunk, step - 1], y_recv.at[chunk, step - 1], row_peer(step),
        )

    def high_peers(which):
        return (high_peer, (dp, opposite(1), my), (turned, opposite(1), my))[which]

    def high_part(held, which):
        return (held.at[0, 1 - high], held.at[1, high], held.at[1, 1 - high])[which]

    def z_copy(chunk, which):
        return remote(
            high_part(y_sum.at[chunk], which), z_in.at[chunk, which],
            z_send.at[chunk, which], z_recv.at[chunk, which], high_peers(which),
        )

    def stage_core(chunk):
        core_copy(chunk).wait_recv()
        core_sum[chunk] = (
            grads[chunk, :, :, core].astype(F32) + core_in[chunk].astype(F32)
        ).astype(BF)
        for step in (2, 1, 3):
            y_copy(chunk, step).start()

    def stage_row(chunk):
        total = core_sum[chunk, :, pl.ds(2 * row, 2)].astype(F32)
        for step in (1, 3, 2):
            y_copy(chunk, step).wait_recv()
            total = total + y_in[chunk, step - 1].astype(F32)
        y_sum[chunk] = total.astype(BF)
        for which in range(3):
            z_copy(chunk, which).start()

    def stage_high(chunk):
        total = y_sum[chunk, 0, high].astype(F32)
        for which in (1, 2, 0):
            z_copy(chunk, which).wait_recv()
            total = total + z_in[chunk, which].astype(F32)
        return total * (1.0 / 16.0)

    def store_qkv(chunk):
        columns = pl.ds(pl.multiple_of(chunk * QKV, HEAD), QKV)
        out_qkv[0, :, columns] = stage_high(chunk)

    def back_pair(head, pair):
        tiles = pl.ds(2 * pair, 2)
        columns = pl.ds(pl.multiple_of(head * QKV, HEAD), QKV)
        back = dot(found[head, tiles, :, HEAD:].reshape(2 * PATCH, QKV), w_qkv[:, columns], NT)
        feat_acc[tiles] += back.reshape(2, PATCH, BOTH)

    def d_copy(pair, step):
        lines = pl.ds(pl.multiple_of(lax.rem(my + step, 4) * QUARTER, QUARTER), QUARTER)
        tiles = pl.ds(2 * pair, 2)
        return remote(
            feat_bf.at[tiles, lines], feat_in.at[step - 1, tiles],
            d_send.at[pair, step - 1], d_recv.at[pair, step - 1], x_peer(step),
        )

    def d_start(pair):
        tiles = pl.ds(2 * pair, 2)
        feat_bf[tiles] = feat_acc[tiles].astype(BF)
        for step in (2, 1, 3):
            d_copy(pair, step).start()

    def d_finish(pair):
        for step in (1, 3, 2):
            d_copy(pair, step).wait_recv()
        for slot in (2 * pair, 2 * pair + 1):
            total = feat_acc[slot, mine, :]
            for step in (1, 3, 2):
                total = total + feat_in[step - 1, slot].astype(F32)
            total = total.astype(BF)
            for block in (1, 0):
                @pl.when(moves(slot, block))
                def _():
                    back_out[slot, block] = total[:, block * WIDE : (block + 1) * WIDE]
                    return_copy(slot, block).start()

            @pl.when(jnp.logical_not(crosses(slot)))
            def _():
                out_feat[tile_of(slot)] = total[:, :WIDE]

    def half_core_copy(half):
        return remote(
            half_grad.at[half, :, :, 1 - core], half_in.at[half],
            half_core_send.at[half], half_core_recv.at[half], core_peer,
        )

    def half_row_copy(step):
        to = lax.rem(row + step, 4)
        return remote(
            half_sum.at[to // 2, :, pl.ds(2 * lax.rem(to, 2), 2)], half_y.at[step - 1],
            half_row_send.at[step - 1], half_row_recv.at[step - 1], row_peer(step),
        )

    def half_high_copy(which):
        return remote(
            high_part(half_ysum, which), half_z.at[which],
            half_high_send.at[which], half_high_recv.at[which], high_peers(which),
        )

    def half_begin(half):
        lines = slice(half * HALF_ROWS, (half + 1) * HALF_ROWS)
        for block in range(2):
            half_grad[half, block] = grad_wide[
                lines, block * WIDE : (block + 1) * WIDE
            ].reshape(4, 2, 48, WIDE)
        half_core_copy(half).start()

    def half_stage_core(half):
        half_core_copy(half).wait_recv()
        half_sum[half] = (
            half_grad[half, :, :, core].astype(F32) + half_in[half].astype(F32)
        ).astype(BF)
        for step in (2, 1, 3):
            @pl.when(lax.rem(row + step, 4) // 2 == half)
            def _():
                half_row_copy(step).start()

    def half_stage_row(half):
        @pl.when(row // 2 == half)
        def _():
            total = half_sum[half, :, pl.ds(2 * lax.rem(row, 2), 2)].astype(F32)
            for step in (1, 3, 2):
                half_row_copy(step).wait_recv()
                total = total + half_y[step - 1].astype(F32)
            half_ysum[...] = total.astype(BF)
            for which in range(3):
                half_high_copy(which).start()

    def half_stage_high(half):
        @pl.when(row // 2 == half)
        def _():
            total = half_ysum[0, high].astype(F32)
            for which in (1, 2, 0):
                half_high_copy(which).wait_recv()
                total = total + half_z[which].astype(F32)
            out_out[0] = total * (1.0 / 16.0)

    def weight_piece(head, at):
        grad = found[head, :, :, HEAD:].reshape(HELD * PATCH, QKV)
        lines = pl.ds(pl.multiple_of(at * HALF_ROWS, HALF_ROWS), HALF_ROWS)
        piece = dot(feat_t[lines, :], grad, NN).astype(BF)
        grads[head, at // 2, pl.ds(4 * lax.rem(at, 2), 4)] = piece.reshape(4, 2, 48, QKV)

    def weights(head):
        run(lambda at: weight_piece(head, at), 0, 4)
        core_copy(head).start()
        lines = pl.ds(pl.multiple_of(head * HEAD, HEAD), HEAD)
        grad_wide[lines, :] = dot(
            found[head, :, :, :HEAD].reshape(HELD * PATCH, HEAD),
            cot[...].reshape(HELD * PATCH, BOTH),
            TN,
        ).astype(BF)
        for half in range(2):
            @pl.when(head == 3 * half + 2)
            def _():
                half_begin(half)


    def near_rows(head):
        back_pair(head, 0)

        @pl.when(head == HEADS_HERE - 1)
        def _():
            d_start(0)

    def far_rows(head):
        for which in range(2):
            c_copy(head, which).wait_recv()
        back_pair(head, 1)

        @pl.when(head == HEADS_HERE - 1)
        def _():
            d_start(1)

    def when(least, head, function):
        @pl.when((head >= least) & (head < HEADS_HERE))
        def _():
            function(head)

    def head_step(now):
        when(1, now, lambda head: b_first(head + 2))
        when(1, now + 1, lambda head: run(project, BACKS + HALF * head, BACKS + HALF * head + HALF))
        @pl.when(now >= 3)
        def _():
            stage_core(now - 3)

        when(0, now - 1, attend_head)

        @pl.when(now < 2)
        def _():
            for slot in range(2):
                columns = pl.ds(pl.multiple_of((2 * now + slot) * PATCH, PATCH), PATCH)
                feat_t[:, columns] = feat[2 * now + slot].T

        @pl.when(now >= 5)
        def _():
            stage_row(now - 5)

        @pl.when(now >= 6)
        def _():
            store_qkv(now - 6)

        for later, stage_half in ((5, half_stage_core), (7, half_stage_row)):
            @pl.when(now == later)
            def _():
                stage_half(0)

        when(0, now - 1, near_rows)
        when(0, now - 2, far_rows)
        when(0, now - 2, weights)

    run(head_step, 0, HEADS_HERE + 2)

    half_stage_core(1)
    stage_core(5)
    d_finish(0)
    stage_row(3)
    store_qkv(2)
    d_finish(1)
    stage_row(4)
    half_stage_row(1)
    store_qkv(3)
    half_stage_high(0)
    stage_row(5)
    store_qkv(4)
    half_stage_high(1)
    store_qkv(5)
    for slot, block in MOVED:
        @pl.when(moves(slot, block))
        def _():
            return_copy(slot, block).wait_recv()
            out_feat[sent_tile(slot, block)] = back_in[slot, block]

    for step in range(1, LOADERS):
        for wave in range(WAVES):
            a_copy(wave, step).wait_send()
        i_copy(step).wait_send()
    for step in range(1, 4):
        for pair in range(2):
            d_copy(pair, step).wait_send()
        half_row_copy(step).wait_send()
    for half in range(2):
        half_core_copy(half).wait_send()
    for which in range(3):
        half_high_copy(which).wait_send()
    for slot, block in MOVED:
        @pl.when(moves(slot, block))
        def _():
            for kind in range(WAVES + 1):
                cross_copy(kind, slot, block).wait_send()
            return_copy(slot, block).wait_send()
            for step in range(1, 4):
                spread_copy(WAVES, slot, block, step).wait_send()

        for step in range(1, 4):
            for wave in range(WAVES):
                spread_copy(wave, slot, block, step).wait_send()
    for kind in range(2):
        w_far_copy(kind).wait_send()
        for step in range(4):
            w_core_copy(kind, step).wait_send()
        for step in range(1, 4):
            w_row_copy(kind, step).wait_send()

    def drain(chunk, carry):
        core_copy(chunk).wait_send()
        for which in range(3):
            z_copy(chunk, which).wait_send()
        for step in range(1, 4):
            y_copy(chunk, step).wait_send()
        return carry

    lax.fori_loop(0, CHUNKS, drain, 0)

    def drain_group(group):
        for which in range(2):
            b_copy(group, which).wait_send()

    def drain_head(head):
        for which in range(2):
            c_copy(head, which).wait_send()

    run(drain_group, 0, GROUPS)
    run(drain_head, 0, HEADS_HERE)


def shards(features, segment_ids, owners, w_qkv, w_out, cotangent):
    vmem = pl.BlockSpec(memory_space=pltpu.VMEM)
    hbm = pl.BlockSpec(memory_space=pl.ANY)
    smem = pl.BlockSpec(memory_space=pltpu.SMEM)
    dma = pltpu.SemaphoreType.DMA
    units = (HEADS_HERE, TILES, PATCH, UNIT)
    sums = (GROUPS, TILES, PATCH, QKV)
    return pl.pallas_call(
        branch,
        out_shape=(
            jax.ShapeDtypeStruct((TILES, 32, WIDE), BF),
            jax.ShapeDtypeStruct((1, 48, HEADS_HERE * QKV), F32),
            jax.ShapeDtypeStruct((1, 48, WIDE), F32),
        ),
        in_specs=[smem, hbm, vmem, hbm, hbm, hbm],
        out_specs=(vmem,) * 3,
        scratch_shapes=[
            pltpu.VMEM((TILES, QUARTER, WIDE), BF),
            pltpu.VMEM((BOTH, HEADS_HERE * QKV), BF),
            pltpu.VMEM((HEADS_HERE * HEAD, BOTH), BF),
            dma((3 + HELD,)),
            pltpu.VMEM((HELD, PATCH, BOTH), BF),
            pltpu.VMEM((HELD, PATCH, BOTH), BF),
            pltpu.VMEM((BOTH, HELD * PATCH), BF),
            pltpu.VMEM((GROUPS, HELD, PATCH, QKV), BF),
            pltpu.VMEM((GROUPS, 2, PATCH, QKV), BF),
            pltpu.VMEM((HEADS_HERE, HELD, PATCH, UNIT), BF),
            pltpu.VMEM((CHUNKS, 2, 8, 2, 48, QKV), BF),
            pltpu.VMEM((CHUNKS, 2, 8, 48, QKV), BF),
            pltpu.VMEM((CHUNKS, 2, 8, 48, QKV), BF),
            pltpu.VMEM((CHUNKS, 3, 2, 2, 48, QKV), BF),
            pltpu.VMEM((CHUNKS, 2, 2, 48, QKV), BF),
            pltpu.VMEM((CHUNKS, 3, 48, QKV), BF),
            pltpu.VMEM((2, 2, 4, 2, 48, WIDE), BF),
            pltpu.VMEM((2, 2, 4, 48, WIDE), BF),
            pltpu.VMEM((2, 2, 4, 48, WIDE), BF),
            pltpu.VMEM((3, 2, 2, 48, WIDE), BF),
            pltpu.VMEM((2, 2, 48, WIDE), BF),
            pltpu.VMEM((3, 48, WIDE), BF),
            pltpu.VMEM((WIDE, BOTH), BF),
            pltpu.VMEM((HELD, PATCH, BOTH), F32),
            pltpu.VMEM((HELD, PATCH, BOTH), BF),
            pltpu.VMEM((3, HELD, QUARTER, BOTH), BF),
            pltpu.VMEM((WAVES, LOADERS, QUARTER, WAVE), BF),
            pltpu.VMEM((LOADERS, QUARTER, WAVE), BF),
            pltpu.VMEM((LOADERS, QUARTER, WAVE), BF),
            pltpu.VMEM((LOADERS, TILES, PATCH), jnp.int32),
            pltpu.VMEM((2, PATCH, PATCH), F32),
            dma((2,)), dma((2,)), dma((2, 3)), dma((2, 3)), dma((2, 4)), dma((2, 4)),
            pltpu.VMEM((WAVES, 2, HELD, QUARTER, WAVE), BF),
            pltpu.VMEM((HELD, 2, QUARTER, WIDE), BF),
            pltpu.VMEM((HELD, 2, QUARTER, WIDE), BF),
            dma((WAVES + 2, HELD, 2)), dma((WAVES + 2, HELD, 2)),
            dma((WAVES + 1, HELD, 2, 3)), dma((WAVES + 1, HELD, 2, 3)),
            dma((WAVES, LOADERS - 1)), dma((WAVES, LOADERS - 1)),
            dma((LOADERS - 1,)), dma((LOADERS - 1,)),
            dma((GROUPS, 2)), dma((GROUPS, 2)),
            dma((HEADS_HERE, 2)), dma((HEADS_HERE, 2)),
            dma((2,)), dma((2,)), dma((3,)), dma((3,)), dma((3,)), dma((3,)),
            dma((CHUNKS,)), dma((CHUNKS,)),
            dma((CHUNKS, 3)), dma((CHUNKS, 3)),
            dma((CHUNKS, 3)), dma((CHUNKS, 3)),
            dma((2, 3)), dma((2, 3)),
        ],
        compiler_params=pltpu.CompilerParams(
            collective_id=0, has_side_effects=True, vmem_limit_bytes=60 * 1024 * 1024
        ),
        cost_estimate=pl.CostEstimate(
            flops=14_000_000_000, bytes_accessed=12_000_000, transcendentals=400_000
        ),
    )(owners, features, segment_ids, cotangent, w_qkv, w_out)


def solution(mesh):
    return jax.shard_map(
        shards,
        mesh=mesh,
        in_specs=(
            P("dp", None, "mx"),
            P("dp", None),
            P(),
            P("mx", "my"),
            P("my", "mx"),
            P("dp", None, "mx"),
        ),
        out_specs=(P("dp", "my", "mx"), P("mx", "dp", "my"), P("my", "dp", "mx")),
        check_vma=False,
    )
```
